32 devices in a mesh: ctx: 8 (over z, x), head: 4 (over y, core).
Axes of the slice: x: 2, y: 2, z: 4, core: 2. Of those that a mesh axis runs over, the one named last changes fastest.
Arguments:
- query_tokens: bfloat16 [2, 2048, 4, 512], P(None, 'ctx', 'head'), may hold values from -6 to 6
- key_tokens: bfloat16 [2048, 4, 512], P('ctx', 'head'), may hold values from -6 to 6
- value_tokens: bfloat16 [2048, 4, 512], P('ctx', 'head'), may hold values from -6 to 6
- log_rate: float32 [4, 2048], P('head', 'ctx'), may hold values from -1.5 to 0.5
- fast_weights: float32 [4, 3, 512, 512], P('head'), may hold values from -0.25 to 0.25
- norm_gain: float32 [4, 512], P('head'), may hold values from 0.5 to 1.5
- out_grad: bfloat16 [2, 2048, 4, 512], P(None, 'ctx', 'head'), may hold values from -0.75 to 0.75
Outputs:
- grad_query: bfloat16 [2, 2048, 4, 512], P(None, 'ctx', 'head')
- grad_key: bfloat16 [2048, 4, 512], P('ctx', 'head')
- grad_value: bfloat16 [2048, 4, 512], P('ctx', 'head')
- grad_rate: float32 [4, 2048], P('head', 'ctx')
- grad_weights: float32 [4, 3, 512, 512], P('head', None, 'ctx')
- grad_gain: float32 [4, 512], P('head', 'ctx')
The draws below stay inside these ranges and needn't reach their ends.
All inputs are finite; a program needn't handle non-finite values.
Results may differ from the reference program's by a relative error of at most 0.0012.
Values sent between devices are 32-bit elements; how exact they have to be, the bound alone decides.
No kernel may reach another device: no remote copies, remote signals or barrier semaphores. Data moves between devices by JAX's collectives and lax.ppermute only.
A program may use at most 128 MiB of HBM per device.

```python
import jax
import jax.numpy as jnp
from jax import lax

D = 512
H = 512
BLOCKS = 2
BLOCK = 2048
HEADS = 4


def block_scale(stream_key, extent, shards, smallest, top_value):
    def one(axis_at, parts):
        steps = jax.random.uniform(jax.random.fold_in(jax.random.fold_in(stream_key, 6), axis_at), (parts,), jnp.float32, smallest / len(shards), top_value / len(shards))
        return jnp.repeat(jnp.exp(steps), extent[axis_at] // parts).reshape((-1,) + (1,) * (len(extent) - axis_at - 1))

    gain = one(*shards[0])
    for cut in shards[1:]:
        gain = gain * one(*cut)
    return gain


def scatter_about(stream_key, shape, scale, bound, shards=(), kind=jnp.bfloat16):
    values = scale * jax.random.normal(stream_key, shape, jnp.float32)
    if shards:
        values = values * block_scale(stream_key, shape, shards, -0.22, 0.18)
    return jnp.clip(values, -bound, bound).astype(kind)


def setup_inputs(seed: int = 0) -> dict:
    keys = jax.random.split(jax.random.key(seed), 8)
    query_tokens = scatter_about(keys[0], (BLOCKS, BLOCK, HEADS, D), 1.0, 6.0, ((1, 8), (2, 4)))
    key_tokens = scatter_about(keys[1], (BLOCK, HEADS, D), 1.0, 6.0, ((0, 8), (1, 4)))
    value_tokens = scatter_about(keys[2], (BLOCK, HEADS, D), 1.0, 6.0, ((0, 8), (1, 4)))
    log_rate = jnp.clip(-1.5 + 2.0 * jax.random.uniform(keys[3], (HEADS, BLOCK), jnp.float32) ** block_scale(keys[3], (HEADS, BLOCK), ((0, 4), (1, 8)), -0.2, 0.2), -1.5, 0.5)
    fast_weights = scatter_about(keys[4], (HEADS, 3, H, D), D ** -0.5, 0.25, ((0, 4),), jnp.float32)
    norm_gain = jnp.clip(1.0 + 0.1 * jax.random.normal(keys[5], (HEADS, D), jnp.float32), 0.5, 1.5)
    out_grad = scatter_about(keys[6], (BLOCKS, BLOCK, HEADS, D), 0.125, 0.75, ((1, 8), (2, 4)))
    return {"query_tokens": query_tokens, "key_tokens": key_tokens, "value_tokens": value_tokens, "log_rate": log_rate, "fast_weights": fast_weights, "norm_gain": norm_gain, "out_grad": out_grad}


EPSILON = 1e-06
PRECISE = lax.Precision.HIGHEST

def apply_fast(weights, inputs):
    gate_pre = jnp.dot(inputs, weights[0].T, precision=PRECISE, preferred_element_type=jnp.float32)
    up_pre = jnp.dot(inputs, weights[1].T, precision=PRECISE, preferred_element_type=jnp.float32)
    hidden = jax.nn.silu(gate_pre) * up_pre
    return jnp.dot(hidden, weights[2], precision=PRECISE, preferred_element_type=jnp.float32)

def update_grad(weights, key_rows, value_rows, rate_log, factor):

    def update_loss(inner):
        rate = jnp.exp(rate_log) * factor
        return -jnp.sum(rate[:, None] * apply_fast(inner, key_rows) * value_rows)
    return jax.grad(update_loss)(weights)

def renorm(update, anchor):
    target = jnp.sqrt(lax.optimization_barrier(jnp.sum(anchor * anchor, axis=-1)) + EPSILON)
    actual = jnp.sqrt(lax.optimization_barrier(jnp.sum(update * update, axis=-1)) + EPSILON)
    return update * (target / actual)[..., None]

def head_forward(weights, queries, key_rows, value_rows, rate_log):
    factor = (BLOCK * D) ** (-0.5)
    grad_now = update_grad(weights, key_rows, value_rows, rate_log, factor)
    new_weights = renorm(weights - grad_now, weights)
    return jnp.stack([apply_fast(weights, queries[0]), apply_fast(new_weights, queries[1])])

def reference(query_tokens, key_tokens, value_tokens, log_rate, fast_weights, norm_gain, out_grad):
    queries = jnp.transpose(query_tokens.astype(jnp.float32), (2, 0, 1, 3))
    key_rows = jnp.transpose(key_tokens.astype(jnp.float32), (1, 0, 2))
    value_rows = jnp.transpose(value_tokens.astype(jnp.float32), (1, 0, 2))
    cotan = jnp.transpose(out_grad.astype(jnp.float32), (2, 0, 1, 3))

    def forward(queries, key_rows, value_rows, rate_log, weights, gains):

        def one_head(items):
            return head_forward(items[0], items[1], items[2], items[3], items[4])
        outputs = lax.map(one_head, (weights, queries, key_rows, value_rows, rate_log))
        inverse = 1.0 / jnp.sqrt(lax.optimization_barrier(jnp.mean(outputs * outputs, axis=(0, 3))) + EPSILON)
        return outputs * gains[:, None, None, :] * inverse[None, :, :, None]
    normed, backward = jax.vjp(forward, queries, key_rows, value_rows, log_rate, fast_weights, norm_gain)
    grads = backward(cotan)
    return (jnp.transpose(grads[0], (1, 2, 0, 3)).astype(jnp.bfloat16), jnp.transpose(grads[1], (1, 0, 2)).astype(jnp.bfloat16), jnp.transpose(grads[2], (1, 0, 2)).astype(jnp.bfloat16), grads[3], grads[4], grads[5])
```

```python
from functools import partial

import jax
import jax.numpy as jnp
import numpy as np
from jax import lax
from jax.experimental import pallas as pl
from jax.experimental.pallas import tpu as pltpu
from jax.sharding import PartitionSpec as P

EPSILON = 1e-06
SETS = 2
VMEM_BYTES = 48 * 1024 * 1024
f32, bf16 = jnp.float32, jnp.bfloat16


def ring_order(count):
    width = max(w for w in range(1, count + 1) if count % w == 0 and w * w <= count)
    height = count // width
    if width == 1 or height % 2:
        return list(range(count))
    order = [0]
    for row in range(height):
        columns = range(1, width) if row % 2 == 0 else range(width - 1, 0, -1)
        order += [row * width + column for column in columns]
    return order + [row * width for row in range(height - 1, 0, -1)]


def ring_tables(count, heads):
    order = ring_order(count)
    pairs = []
    for head in range(heads):
        way = order if head % 2 == 0 else order[::-1]
        for at in range(count):
            pairs.append((way[at] * heads + head, way[(at + 1) % count] * heads + head))
    owner = np.zeros((2, count, count), np.int32)
    for parity in range(2):
        way = order if parity == 0 else order[::-1]
        for at in range(count):
            for step in range(count):
                owner[parity, way[at], step] = way[(at - 1 - step) % count]
    return pairs, owner


def pair(x):
    high = x.astype(bf16)
    return high, (x - high.astype(f32)).astype(bf16)


def nt(a, b):
    return lax.dot_general(a, b, (((1,), (1,)), ((), ())), preferred_element_type=f32)


def nn(a, b):
    return lax.dot_general(a, b, (((1,), (0,)), ((), ())), preferred_element_type=f32)


def tn(a, b):
    return lax.dot_general(a, b, (((0,), (0,)), ((), ())), preferred_element_type=f32)


def three(dot, a, b):
    (a_high, a_low), (b_high, b_low) = a, b
    return dot(a_high, b_high) + (dot(a_high, b_low) + dot(a_low, b_high))


def rows_by(x, mats):
    pairs = [pair(m) for m in mats]
    stacked = jnp.concatenate([p[0] for p in pairs] + [p[1] for p in pairs], axis=0)
    both = nt(x, stacked)
    half = both.shape[1] // 2
    total = both[:, :half] + both[:, half:]
    rows = mats[0].shape[0]
    return [total[:, i * rows : (i + 1) * rows] for i in range(len(mats))]


def sums_by(parts, x):
    pairs = [pair(m) for m in parts]
    stacked = jnp.concatenate([p[0] for p in pairs] + [p[1] for p in pairs], axis=1)
    both = tn(stacked, x)
    half = both.shape[0] // 2
    total = both[:half] + both[half:]
    rows = parts[0].shape[1]
    return [total[i * rows : (i + 1) * rows] for i in range(len(parts))]


def silu_parts(gate):
    sig = 1.0 / (1.0 + jnp.exp(-gate))
    act = gate * sig
    return sig, act, sig + act * (1.0 - sig)


def to_columns(rows):
    count, tokens = rows.shape
    if count < 128:
        rows = jnp.concatenate([rows, jnp.zeros((128 - count, tokens), f32)], axis=0)
    turned = jnp.transpose(rows)
    return [turned[:, i : i + 1] for i in range(count)]


def to_rows(columns):
    tokens = columns[0].shape[0]
    lane = lax.broadcasted_iota(jnp.int32, (tokens, 128), 1)
    packed = jnp.zeros((tokens, 128), f32)
    for i, column in enumerate(columns):
        packed = jnp.where(lane == i, column, packed)
    return jnp.transpose(packed)[:8]


def minus_rate(rate_ref, factor):
    return -jnp.exp(to_columns(rate_ref[...])[0]) * factor


def update_kernel(factor, chunks, sets, owner_ref, weights_ref, key_ref, value_ref, rate_ref, placed_ref, *parts_ref):
    rows = weights_ref.shape[1] // chunks
    piece = rows // sets
    for step in range(chunks):
        placed_ref[:, step * rows : (step + 1) * rows, :] = weights_ref[:, pl.ds(pl.multiple_of(owner_ref[step] * rows, rows), rows), :]
    keys, values = key_ref[...], value_ref[...]
    gate, up = rows_by(keys, [placed_ref[0], placed_ref[1]])
    (back,) = rows_by(values, [placed_ref[2]])
    rate = minus_rate(rate_ref, factor)
    _, act, slope = silu_parts(gate)
    back = back * rate
    grad_gate, grad_up = sums_by([back * up * slope, back * act], keys)
    (grad_down,) = sums_by([act * up * rate], values)
    for step in range(chunks):
        for part in range(sets):
            at = step * rows + part * piece
            out = parts_ref[step * sets + part]
            out[0] = grad_gate[at : at + piece]
            out[1] = grad_up[at : at + piece]
            out[2] = grad_down[at : at + piece]


def scales(update, anchor):
    target = jnp.sqrt(jnp.sum(anchor * anchor, axis=-1, keepdims=True) + EPSILON)
    actual = jnp.sqrt(jnp.sum(update * update, axis=-1, keepdims=True) + EPSILON)
    return target, actual


def renorm_kernel(arrived_ref, mine_ref, anchor_ref, update_ref, new_ref):
    anchor = anchor_ref[...]
    update = anchor - (arrived_ref[...] + mine_ref[...])
    target, actual = scales(update, anchor)
    update_ref[...] = update
    new_ref[...] = update * (target / actual)


def renorm_back_kernel(sets, anchor_ref, *refs):
    arrived, mine, updates = refs[:sets], refs[sets : 2 * sets], refs[2 * sets : 3 * sets]
    turned_ref, direct_ref = refs[3 * sets :]
    piece = updates[0].shape[1]
    for part in range(sets):
        at = pl.ds(part * piece, piece)
        anchor = anchor_ref[:, at, :]
        update = updates[part][...]
        cot = arrived[part][...] + mine[part][...]
        target, actual = scales(update, anchor)
        inner = jnp.sum(update * cot, axis=-1, keepdims=True)
        ratio = target / actual
        update_cot = ratio * cot - update * (inner * ratio / (actual * actual))
        turned_ref[:, at, :] = -update_cot
        direct_ref[:, at, :] = update_cot + anchor * (inner / (actual * target))


def forward_pass(queries, gate_mat, up_mat, down_mat):
    gate, up = rows_by(queries, [gate_mat, up_mat])
    _, act, _ = silu_parts(gate)
    out = three(nn, pair(act * up), pair(down_mat))
    return gate, up, out


def norm_sums(out, cotan, gain):
    return [jnp.sum(out * out, axis=1, keepdims=True), jnp.sum(gain * cotan * out, axis=1, keepdims=True)]


def forward_one_kernel(query_ref, cotan_ref, gain_ref, weights_ref, gate_ref, up_ref, out_ref, stats_ref):
    gate, up, out = forward_pass(query_ref[...], weights_ref[0], weights_ref[1], weights_ref[2])
    gate_ref[...] = gate
    up_ref[...] = up
    out_ref[...] = out
    stats_ref[...] = to_rows(norm_sums(out, cotan_ref[...].astype(f32), gain_ref[...]))


def forward_two_kernel(count, query_ref, cotan_ref, gain_ref, other_ref, *refs):
    chunks, (weights_ref, gate_ref, up_ref, out_ref, stats_ref) = refs[:count], refs[count:]
    piece = chunks[0].shape[1]
    for i, chunk in enumerate(chunks):
        weights_ref[:, i * piece : (i + 1) * piece, :] = chunk[...]
    gate, up, out = forward_pass(query_ref[...], weights_ref[0], weights_ref[1], weights_ref[2])
    gate_ref[...] = gate
    up_ref[...] = up
    out_ref[...] = out
    mine = to_rows([jnp.zeros((out.shape[0], 1), f32)] * 2 + norm_sums(out, cotan_ref[...].astype(f32), gain_ref[...]))
    stats_ref[...] = mine + other_ref[...]


def backward_kernel(first, width, count, query_ref, cotan_ref, gain_ref, stats_ref, weights_ref, gate_ref, up_ref, out_ref, grad_gate_ref, grad_up_ref, gain_term_ref, *parts_ref):
    columns = to_columns(stats_ref[...])
    square, product = columns[first], columns[first + 1]
    inverse = 1.0 / jnp.sqrt(square / width + EPSILON)
    out, cotan = out_ref[...], cotan_ref[...].astype(f32)
    grad_out = gain_ref[...] * cotan * inverse - out * (inverse * inverse * inverse * product / width)
    gain_term_ref[...] = jnp.sum(cotan * out * inverse, axis=0, keepdims=True)
    up = up_ref[...]
    _, act, slope = silu_parts(gate_ref[...])
    grad_out = pair(grad_out)
    back = three(nt, grad_out, pair(weights_ref[2]))
    grad_gate, grad_up = back * up * slope, back * act
    grad_gate_ref[...] = grad_gate
    grad_up_ref[...] = grad_up
    sum_gate, sum_up = sums_by([grad_gate, grad_up], query_ref[...])
    sum_down = three(tn, pair(act * up), grad_out)
    piece = sum_gate.shape[0] // count
    for i in range(count):
        at = slice(i * piece, (i + 1) * piece)
        parts_ref[i][0] = sum_gate[at]
        parts_ref[i][1] = sum_up[at]
        parts_ref[i][2] = sum_down[at]


def query_grad_kernel(grad_gate_ref, grad_up_ref, weights_ref, out_ref):
    total = three(nn, pair(grad_gate_ref[...]), pair(weights_ref[0]))
    total = total + three(nn, pair(grad_up_ref[...]), pair(weights_ref[1]))
    out_ref[...] = total.astype(bf16)


def second_order(keys, values, rate, weights, turns):
    gate, up, gate_turn, up_turn = rows_by(keys, [weights[0], weights[1], turns[0], turns[1]])
    back, back_turn = rows_by(values, [weights[2], turns[2]])
    back, back_turn = back * rate, back_turn * rate
    sig, act, slope = silu_parts(gate)
    bend = sig * (1.0 - sig) * (2.0 + gate * (1.0 - 2.0 * sig))
    hidden_turn = slope * gate_turn * up + act * up_turn
    cot_gate = back * (bend * gate_turn * up + slope * up_turn) + back_turn * up * slope
    cot_up = back * slope * gate_turn + back_turn * act
    return act * up, hidden_turn, cot_gate, cot_up, back * slope * up, back * act


def update_back_kernel(factor, key_ref, value_ref, rate_ref, weights_ref, turn_ref, gathered_ref, gain_ref, out_ref):
    keys, values = key_ref[...], value_ref[...]
    rate = minus_rate(rate_ref, factor)
    rows = weights_ref.shape[1]
    _, hidden_turn, cot_gate, cot_up, _, _ = second_order(keys, values, rate, [weights_ref[i] for i in range(3)], [turn_ref[i] for i in range(3)])
    sum_gate, sum_up = sums_by([cot_gate, cot_up], keys)
    (sum_down,) = sums_by([hidden_turn * rate], values)
    out_ref[0:rows] = sum_gate + gathered_ref[0]
    out_ref[rows : 2 * rows] = sum_up + gathered_ref[1]
    out_ref[2 * rows : 3 * rows] = sum_down + gathered_ref[2]
    out_ref[3 * rows :] = gain_ref[...]


def token_kernel(factor, key_ref, value_ref, rate_ref, weights_ref, *refs):
    turns_ref, (grad_key_ref, grad_value_ref, grad_rate_ref) = refs[:-3], refs[-3:]
    keys, values = key_ref[...], value_ref[...]
    rate = minus_rate(rate_ref, factor)
    weights = [weights_ref[i] for i in range(3)]
    turns = [jnp.concatenate([t[i] for t in turns_ref], axis=0) for i in range(3)]
    hidden, hidden_turn, cot_gate, cot_up, cot_gate_turn, cot_up_turn = second_order(keys, values, rate, weights, turns)
    grad_key = three(nn, pair(cot_gate), pair(weights[0])) + three(nn, pair(cot_up), pair(weights[1]))
    grad_key = grad_key + three(nn, pair(cot_gate_turn), pair(turns[0])) + three(nn, pair(cot_up_turn), pair(turns[1]))
    grad_key_ref[...] = grad_key.astype(bf16)
    grad_value = rate * (three(nn, pair(hidden_turn), pair(weights[2])) + three(nn, pair(hidden), pair(turns[2])))
    grad_value_ref[...] = grad_value.astype(bf16)
    grad_rate_ref[...] = to_rows([jnp.sum(grad_value * values.astype(f32), axis=1, keepdims=True)])[:1]


def call(kernel, outs, *args, scalars=0, name=None):
    in_specs = [pl.BlockSpec(memory_space=pltpu.SMEM)] * scalars + [pl.BlockSpec(memory_space=pltpu.VMEM)] * (len(args) - scalars)
    return pl.pallas_call(
        kernel,
        out_shape=[jax.ShapeDtypeStruct(shape, dtype) for shape, dtype in outs],
        in_specs=in_specs,
        out_specs=[pl.BlockSpec(memory_space=pltpu.VMEM)] * len(outs),
        compiler_params=pltpu.CompilerParams(vmem_limit_bytes=VMEM_BYTES),
        name=name,
    )(*args)


def local(chunks, heads, query_tokens, key_tokens, value_tokens, log_rate, fast_weights, norm_gain, out_grad):
    pairs, owner_table = ring_tables(chunks, heads)
    owner = jnp.asarray(owner_table)[lax.axis_index("head") % 2, lax.axis_index("ctx")]

    def send(x):
        return lax.ppermute(x, ("ctx", "head"), pairs)

    weights = fast_weights[0]
    query_one, query_two = query_tokens[0, :, 0, :], query_tokens[1, :, 0, :]
    cotan_one, cotan_two = out_grad[0, :, 0, :], out_grad[1, :, 0, :]
    keys, values = key_tokens[:, 0, :], value_tokens[:, 0, :]
    tokens, width = keys.shape
    hidden = weights.shape[1]
    rows = hidden // chunks
    piece = rows // SETS
    factor = (tokens * chunks * width) ** (-0.5)
    norm_width = heads * width
    token_f32, whole = ((tokens, width), f32), ((3, hidden, width), f32)
    small, chunk = ((3, piece, width), f32), ((3, rows, width), f32)
    hidden_f32 = ((tokens, hidden), f32)
    stats_shape = ((8, tokens), f32)

    def scatter(parts):
        totals = list(parts[0])
        for step in range(chunks - 1):
            totals = [send(t) for t in totals]
            if step < chunks - 2:
                totals = [t + p for t, p in zip(totals, parts[step + 1])]
        return totals

    def grid_of(flat):
        return [flat[i * SETS : (i + 1) * SETS] for i in range(chunks)]

    placed, *parts = call(
        partial(update_kernel, factor, chunks, SETS), [whole] + [small] * (chunks * SETS), owner, weights, keys, values, log_rate, scalars=1, name="update"
    )
    parts = grid_of(parts)
    arrived = scatter(parts)
    gate_one, up_one, out_one, stats_one = call(
        forward_one_kernel, [hidden_f32, hidden_f32, token_f32, stats_shape], query_one, cotan_one, norm_gain, placed, name="forward_one"
    )
    mine = placed[:, hidden - rows :, :]
    updates, news = [], []
    for i in range(SETS):
        update, new = call(renorm_kernel, [small, small], arrived[i], parts[-1][i], mine[:, i * piece : (i + 1) * piece, :], name="renorm")
        updates.append(update)
        news.append(new)
    gathered, held = [], list(news)
    for step in range(chunks - 1):
        held = [send(h) for h in held]
        gathered += held
    gathered += news

    new_weights, gate_two, up_two, out_two, stats = call(
        partial(forward_two_kernel, chunks * SETS),
        [whole, hidden_f32, hidden_f32, token_f32, stats_shape],
        query_two, cotan_two, norm_gain, stats_one, *gathered, name="forward_two",
    )
    stats = lax.psum(stats, "head")
    grad_gate, grad_up, gain_two, *parts = call(
        partial(backward_kernel, 2, norm_width, chunks * SETS), [hidden_f32, hidden_f32, ((1, width), f32)] + [small] * (chunks * SETS),
        query_two, cotan_two, norm_gain, stats, new_weights, gate_two, up_two, out_two, name="backward_two",
    )
    parts = grid_of(parts)
    arrived = scatter(parts)
    (grad_query_two,) = call(query_grad_kernel, [((tokens, width), bf16)], grad_gate, grad_up, new_weights, name="query_two")
    grad_gate, grad_up, gain_one, *direct_parts = call(
        partial(backward_kernel, 0, norm_width, chunks), [hidden_f32, hidden_f32, ((1, width), f32)] + [chunk] * chunks,
        query_one, cotan_one, norm_gain, stats, placed, gate_one, up_one, out_one, name="backward_one",
    )
    (grad_query_one,) = call(query_grad_kernel, [((tokens, width), bf16)], grad_gate, grad_up, placed, name="query_one")

    turn, direct = call(partial(renorm_back_kernel, SETS), [chunk, chunk], mine, *arrived, *parts[-1], *updates, name="renorm_back")
    gain_rows = (gain_one + gain_two).reshape(chunks, width // chunks)[owner]
    gain_rows = jnp.pad(gain_rows[:, None, :], ((0, 0), (0, 7), (0, width - width // chunks)))
    packed = ((3 * rows + 8, width), f32)

    def back_at(step, turned):
        (out,) = call(
            partial(update_back_kernel, factor), [packed], keys, values, log_rate, placed[:, step * rows : (step + 1) * rows, :], turned,
            direct_parts[step], gain_rows[step], name="update_back",
        )
        return out

    turns, total, held = [], None, turn
    for step in range(chunks - 1):
        held = send(held)
        turns.append(held)
        mine_now = back_at(step, held)
        total = send(mine_now if total is None else total + mine_now)
    turns.append(turn)
    grad_key, grad_value, grad_rate = call(
        partial(token_kernel, factor), [((tokens, width), bf16), ((tokens, width), bf16), ((1, tokens), f32)],
        keys, values, log_rate, placed, *turns, name="tokens",
    )
    total = total + back_at(chunks - 1, turn)
    grad_weights = total[: 3 * rows].reshape(3, rows, width) + direct
    grad_query = jnp.stack([grad_query_one, grad_query_two])[:, :, None, :]
    return (
        grad_query, grad_key[:, None, :], grad_value[:, None, :], grad_rate, grad_weights[None], total[3 * rows : 3 * rows + 1, : width // chunks],
    )


def solution(mesh):
    placed = (
        P(None, "ctx", "head", None),
        P("ctx", "head", None),
        P("ctx", "head", None),
        P("head", "ctx"),
        P("head", None, None, None),
        P("head", None),
        P(None, "ctx", "head", None),
    )
    return jax.shard_map(
        partial(local, mesh.shape["ctx"], mesh.shape["head"]),
        mesh=mesh,
        in_specs=placed,
        out_specs=(
            P(None, "ctx", "head", None),
            P("ctx", "head", None),
            P("ctx", "head", None),
            P("head", "ctx"),
            P("head", None, "ctx", None),
            P("head", "ctx"),
        ),
        check_vma=False,
    )
```

```python
from functools import partial

import jax
import jax.numpy as jnp
from jax import lax
from jax.experimental import pallas as pl
from jax.experimental.pallas import tpu as pltpu
from jax.sharding import PartitionSpec as P

EPSILON = 1e-06
VMEM_BYTES = 16 * 1024 * 1024
FIRST_VMEM, REST_VMEM = 60 * 1024 * 1024, 52 * 1024 * 1024
f32, bf16 = jnp.float32, jnp.bfloat16


def ring_order(count):
    width = max(w for w in range(1, count + 1) if count % w == 0 and w * w <= count)
    height = count // width
    if width == 1 or height % 2:
        return list(range(count))
    order = [0]
    for row in range(height):
        columns = range(1, width) if row % 2 == 0 else range(width - 1, 0, -1)
        order += [row * width + column for column in columns]
    return order + [row * width for row in range(height - 1, 0, -1)]


def ring_pairs(count, heads):
    order, pairs = ring_order(count), []
    for head in range(heads):
        way = order if head % 2 == 0 else order[::-1]
        pairs += [(way[at] * heads + head, way[(at + 1) % count] * heads + head) for at in range(count)]
    return pairs


def owner_at(order, step):
    device, sign = lax.axis_index("ctx"), 1 - 2 * lax.rem(lax.axis_index("head"), 2)
    count = len(order)
    at = sum(jnp.where(device == name, place, 0) for place, name in enumerate(order))
    place = lax.rem(at - sign * (1 + step) + 2 * count, count)
    return sum(jnp.where(place == i, name, 0) for i, name in enumerate(order))


def pair(x):
    high = x.astype(bf16)
    return high, (x - high.astype(f32)).astype(bf16)


def nt(a, b):
    return lax.dot_general(a, b, (((1,), (1,)), ((), ())), preferred_element_type=f32)


def nn(a, b):
    return lax.dot_general(a, b, (((1,), (0,)), ((), ())), preferred_element_type=f32)


def tn(a, b):
    return lax.dot_general(a, b, (((0,), (0,)), ((), ())), preferred_element_type=f32)


def three(dot, a, b):
    (a_high, a_low), (b_high, b_low) = a, b
    return dot(a_high, b_high) + (dot(a_high, b_low) + dot(a_low, b_high))


def rows_by(x, mats):
    pairs = [pair(m) for m in mats]
    stacked = jnp.concatenate([p[0] for p in pairs] + [p[1] for p in pairs], axis=0)
    both = nt(x, stacked)
    half = both.shape[1] // 2
    total = both[:, :half] + both[:, half:]
    rows = mats[0].shape[0]
    return [total[:, i * rows : (i + 1) * rows] for i in range(len(mats))]


def sums_by(parts, x):
    pairs = [pair(m) for m in parts]
    stacked = jnp.concatenate([p[0] for p in pairs] + [p[1] for p in pairs], axis=1)
    both = tn(stacked, x)
    half = both.shape[0] // 2
    total = both[:half] + both[half:]
    rows = parts[0].shape[1]
    return [total[i * rows : (i + 1) * rows] for i in range(len(parts))]


def silu_parts(gate):
    sig = 1.0 / (1.0 + jnp.exp(-gate))
    act = gate * sig
    return sig, act, sig + act * (1.0 - sig)


def to_columns(rows):
    count, tokens = rows.shape
    if count < 128:
        rows = jnp.concatenate([rows, jnp.zeros((128 - count, tokens), f32)], axis=0)
    turned = jnp.transpose(rows)
    return [turned[:, i : i + 1] for i in range(count)]


def to_rows(columns):
    tokens = columns[0].shape[0]
    lane = lax.broadcasted_iota(jnp.int32, (tokens, 128), 1)
    packed = jnp.zeros((tokens, 128), f32)
    for i, column in enumerate(columns):
        packed = jnp.where(lane == i, column, packed)
    return jnp.transpose(packed)[:8]


def minus_rate(rate_ref, factor):
    return -jnp.exp(to_columns(rate_ref[...])[0]) * factor


def write_parts(parts_ref, sums, steps):
    rows = sums[0].shape[0] // steps
    for step in range(steps):
        for i, total in enumerate(sums):
            parts_ref[3 * step + i][...] = total[step * rows : (step + 1) * rows]


def update_kernel(factor, order, first, steps, weights_ref, key_ref, value_ref, rate_ref, *refs):
    placed_ref, key_here, value_here, weight_sems, token_sems = refs[-5:]
    parts_ref, chunks_ref = refs[: 3 * steps], refs[3 * steps : -5]
    rows = weights_ref.shape[1] // len(order)
    copies = [pltpu.make_async_copy(key_ref, key_here, token_sems.at[0])]
    copies[0].start()
    for step in range(steps):
        source = weights_ref.at[:, pl.ds(pl.multiple_of(owner_at(order, first + step) * rows, rows), rows), :]
        copy = pltpu.make_async_copy(source, placed_ref.at[:, pl.ds(step * rows, rows), :], weight_sems.at[step])
        copy.start()
        copies.append(copy)
    copy = pltpu.make_async_copy(value_ref, value_here, token_sems.at[1])
    copy.start()
    rate = minus_rate(rate_ref, factor)
    for copy in copies + [copy]:
        copy.wait()
    keys, values = key_here[...], value_here[...]
    gate, up = rows_by(keys, [placed_ref[0], placed_ref[1]])
    (back,) = rows_by(values, [placed_ref[2]])
    _, act, slope = silu_parts(gate)
    back = back * rate
    grad_gate, grad_up = sums_by([back * up * slope, back * act], keys)
    (grad_down,) = sums_by([act * up * rate], values)
    write_parts(parts_ref, [grad_gate, grad_up, grad_down], steps)
    for step, chunk_ref in enumerate(chunks_ref):
        chunk_ref[...] = placed_ref[:, step * rows : (step + 1) * rows, :]


def scales(update, anchor):
    target = jnp.sqrt(jnp.sum(anchor * anchor, axis=-1, keepdims=True) + EPSILON)
    actual = jnp.sqrt(jnp.sum(update * update, axis=-1, keepdims=True) + EPSILON)
    return target, actual


def renorm_kernel(which, arrived_ref, mine_ref, anchor_ref, update_ref, new_ref):
    anchor = anchor_ref[which]
    update = anchor - (arrived_ref[...] + mine_ref[...])
    target, actual = scales(update, anchor)
    update_ref[...] = update
    new_ref[...] = update * (target / actual)


def renorm_back_kernel(anchor_ref, gain_one_ref, gain_two_ref, *refs):
    arrived, mine, updates, (turned_ref, direct_ref, gain_ref) = refs[:3], refs[3:6], refs[6:9], refs[9:]
    for i in range(3):
        anchor, update, cot = anchor_ref[i], updates[i][...], arrived[i][...] + mine[i][...]
        target, actual = scales(update, anchor)
        inner = jnp.sum(update * cot, axis=-1, keepdims=True)
        ratio = target / actual
        update_cot = ratio * cot - update * (inner * ratio / (actual * actual))
        turned_ref[i] = -update_cot
        direct_ref[i] = update_cot + anchor * (inner / (actual * target))
    gain_ref[...] = gain_one_ref[...] + gain_two_ref[...]


def forward_pass(queries, gate_mat, up_mat, down_mat):
    gate, up = rows_by(queries, [gate_mat, up_mat])
    _, act, _ = silu_parts(gate)
    out = three(nn, pair(act * up), pair(down_mat))
    return gate, up, out


def norm_sums(out, cotan, gain):
    return [jnp.sum(out * out, axis=1, keepdims=True), jnp.sum(gain * cotan * out, axis=1, keepdims=True)]


def forward_kernel(count, other, query_ref, cotan_ref, gain_ref, *refs):
    if other:
        other_ref, refs = refs[0], refs[1:]
    chunks, (weights_ref, gate_ref, up_ref, out_ref, stats_ref) = refs[:count], refs[count:]
    rows = weights_ref.shape[1] // (count if len(chunks[0].shape) == 3 else count // 3)
    for i, chunk in enumerate(chunks):
        if len(chunk.shape) == 3:
            weights_ref[:, i * rows : (i + 1) * rows, :] = chunk[...]
        else:
            weights_ref[i % 3, i // 3 * rows : (i // 3 + 1) * rows, :] = chunk[...]
    gate, up, out = forward_pass(query_ref[...], weights_ref[0], weights_ref[1], weights_ref[2])
    gate_ref[...] = gate
    up_ref[...] = up
    out_ref[...] = out
    sums = norm_sums(out, cotan_ref[...].astype(f32), gain_ref[...])
    if other:
        stats_ref[...] = to_rows([jnp.zeros((out.shape[0], 1), f32)] * 2 + sums) + other_ref[...]
    else:
        stats_ref[...] = to_rows(sums)


def backward_kernel(first, width, chunks, split, query_ref, cotan_ref, gain_ref, stats_ref, weights_ref, gate_ref, up_ref, out_ref, grad_gate_ref, grad_up_ref, gain_term_ref, *parts_ref):
    columns = to_columns(stats_ref[...])
    square, product = columns[first], columns[first + 1]
    inverse = 1.0 / jnp.sqrt(square / width + EPSILON)
    out, cotan = out_ref[...], cotan_ref[...].astype(f32)
    grad_out = gain_ref[...] * cotan * inverse - out * (inverse * inverse * inverse * product / width)
    gain_term_ref[...] = jnp.sum(cotan * out * inverse, axis=0, keepdims=True)
    up = up_ref[...]
    _, act, slope = silu_parts(gate_ref[...])
    grad_out = pair(grad_out)
    back = three(nt, grad_out, pair(weights_ref[2]))
    grad_gate, grad_up = back * up * slope, back * act
    grad_gate_ref[...] = grad_gate
    grad_up_ref[...] = grad_up
    sum_gate, sum_up = sums_by([grad_gate, grad_up], query_ref[...])
    sum_down = three(tn, pair(act * up), grad_out)
    if split:
        write_parts(parts_ref, [sum_gate, sum_up, sum_down], chunks)
    else:
        rows = sum_gate.shape[0] // chunks
        for step in range(chunks):
            for i, total in enumerate((sum_gate, sum_up, sum_down)):
                parts_ref[step][i] = total[step * rows : (step + 1) * rows]


def query_grad_kernel(grad_gate_ref, grad_up_ref, weights_ref, out_ref):
    total = three(nn, pair(grad_gate_ref[...]), pair(weights_ref[0]))
    total = total + three(nn, pair(grad_up_ref[...]), pair(weights_ref[1]))
    out_ref[...] = total.astype(bf16)


def second_order(keys, values, rate, weights, turns):
    gate, up, gate_turn, up_turn = rows_by(keys, [weights[0], weights[1], turns[0], turns[1]])
    back, back_turn = rows_by(values, [weights[2], turns[2]])
    back, back_turn = back * rate, back_turn * rate
    sig, act, slope = silu_parts(gate)
    bend = sig * (1.0 - sig) * (2.0 + gate * (1.0 - 2.0 * sig))
    hidden_turn = slope * gate_turn * up + act * up_turn
    cot_gate = back * (bend * gate_turn * up + slope * up_turn) + back_turn * up * slope
    cot_up = back * slope * gate_turn + back_turn * act
    return act * up, hidden_turn, cot_gate, cot_up, back * slope * up, back * act


def update_back_kernel(factor, order, step, first, last, key_ref, value_ref, rate_ref, weights_ref, turn_ref, gathered_ref, gain_ref, *refs):
    if first:
        direct_ref, refs = refs[0], refs[1:]
    else:
        before_key_ref, before_value_ref, refs = refs[0], refs[1], refs[2:]
    out_ref, grad_key_ref, grad_value_ref = refs[:3]
    keys, values = key_ref[...], value_ref[...]
    rate = minus_rate(rate_ref, factor)
    rows = weights_ref.shape[1]
    weights, turns = [weights_ref[i] for i in range(3)], [turn_ref[i] for i in range(3)]
    hidden, hidden_turn, cot_gate, cot_up, cot_gate_turn, cot_up_turn = second_order(keys, values, rate, weights, turns)
    sums = sums_by([cot_gate, cot_up], keys) + sums_by([hidden_turn * rate], values)
    for i, total in enumerate(sums):
        total = total + gathered_ref[i]
        out_ref[i * rows : (i + 1) * rows] = total + direct_ref[i] if first else total
    gain = jnp.broadcast_to(gain_ref[...], (8, gain_ref.shape[1]))
    piece = gain_ref.shape[1] // len(order)
    out_ref[3 * rows :] = pltpu.roll(gain, lax.rem((len(order) - owner_at(order, step)) * piece, gain_ref.shape[1]), 1)
    grad_key = three(nn, pair(jnp.concatenate([cot_gate, cot_up, cot_gate_turn, cot_up_turn], axis=1)), pair(jnp.concatenate([weights[0], weights[1], turns[0], turns[1]], axis=0)))
    grad_value = rate * three(nn, pair(jnp.concatenate([hidden_turn, hidden], axis=1)), pair(jnp.concatenate([weights[2], turns[2]], axis=0)))
    if not first:
        grad_key, grad_value = grad_key + before_key_ref[...], grad_value + before_value_ref[...]
    grad_key_ref[...] = grad_key.astype(grad_key_ref.dtype)
    grad_value_ref[...] = grad_value.astype(grad_value_ref.dtype)
    if last:
        refs[3][...] = to_rows([jnp.sum(grad_value * values.astype(f32), axis=1, keepdims=True)])[:1]


def finish_kernel(arrived_ref, mine_ref, weights_ref, gain_ref):
    rows = weights_ref.shape[1]
    for i in range(3):
        at = slice(i * rows, (i + 1) * rows)
        weights_ref[i] = arrived_ref[at] + mine_ref[at]
    gain_ref[...] = (arrived_ref[3 * rows :] + mine_ref[3 * rows :])[:1, : gain_ref.shape[1]]


def call(kernel, outs, *args, in_hbm=0, scratch=(), name=None, micros=4, vmem=VMEM_BYTES):
    in_specs = [pl.BlockSpec(memory_space=pl.ANY)] * in_hbm + [pl.BlockSpec(memory_space=pltpu.VMEM)] * (len(args) - in_hbm)
    return pl.pallas_call(
        kernel,
        out_shape=[jax.ShapeDtypeStruct(shape, dtype) for shape, dtype in outs],
        in_specs=in_specs,
        out_specs=[pl.BlockSpec(memory_space=pltpu.VMEM)] * len(outs),
        scratch_shapes=scratch,
        compiler_params=pltpu.CompilerParams(vmem_limit_bytes=vmem),
        cost_estimate=pl.CostEstimate(flops=int(micros * 1e9), transcendentals=0, bytes_accessed=int(micros * 3e6)),
        name=name,
    )(*args)


def local(chunks, heads, query_tokens, key_tokens, value_tokens, log_rate, fast_weights, norm_gain, out_grad):
    order, pairs = ring_order(chunks), ring_pairs(chunks, heads)

    def send(x):
        return lax.ppermute(x, ("ctx", "head"), pairs)

    weights = fast_weights[0]
    query_one, query_two = query_tokens[0, :, 0, :], query_tokens[1, :, 0, :]
    cotan_one, cotan_two = out_grad[0, :, 0, :], out_grad[1, :, 0, :]
    keys, values = key_tokens[:, 0, :], value_tokens[:, 0, :]
    tokens, width = keys.shape
    hidden = weights.shape[1]
    rows = hidden // chunks
    factor = (tokens * chunks * width) ** (-0.5)
    norm_width = heads * width
    token_f32, token_bf16, whole = ((tokens, width), f32), ((tokens, width), bf16), ((3, hidden, width), f32)
    hidden_f32, stats_shape, gain_shape = ((tokens, hidden), f32), ((8, tokens), f32), ((1, width), f32)
    chunk, part, packed = ((3, rows, width), f32), ((rows, width), f32), ((3 * rows + 8, width), f32)

    def scatter(parts):
        totals = list(parts[:3])
        for step in range(chunks - 1):
            totals = [send(t) for t in totals]
            if step < chunks - 2:
                totals = [t + p for t, p in zip(totals, parts[3 * step + 3 :])]
        return totals

    def update(first, steps, keep, vmem):
        return call(
            partial(update_kernel, factor, order, first, steps), [part] * (3 * steps) + ([chunk] * steps if keep else []), weights, keys, values, log_rate,
            in_hbm=3, vmem=vmem, name="update",
            scratch=[pltpu.VMEM((3, steps * rows, width), f32), pltpu.VMEM((tokens, width), bf16), pltpu.VMEM((tokens, width), bf16)]
            + [pltpu.SemaphoreType.DMA((steps,)), pltpu.SemaphoreType.DMA((2,))],
        )

    parts = update(0, 1, True, FIRST_VMEM)
    parts, placed = parts[:3], parts[3:]
    rest = update(1, chunks - 1, True, REST_VMEM)
    parts, placed = parts + rest[: -(chunks - 1)], placed + rest[-(chunks - 1) :]
    arrived = scatter(parts)
    old_weights, gate_one, up_one, out_one, stats_one = call(
        partial(forward_kernel, chunks, False), [whole, hidden_f32, hidden_f32, token_f32, stats_shape], query_one, cotan_one, norm_gain, *placed, name="forward_one"
    )
    updates, gathered = [], []
    for i in range(3):
        new = call(partial(renorm_kernel, i), [part] * 2, arrived[i], parts[i - 3], placed[-1], name="renorm")
        updates.append(new[0])
        gathered.append(new[1])
    held, gathered = gathered, []
    news = held
    for step in range(chunks - 1):
        held = [send(h) for h in held]
        gathered += held
    gathered += news

    new_weights, gate_two, up_two, out_two, stats = call(
        partial(forward_kernel, len(gathered), True), [whole, hidden_f32, hidden_f32, token_f32, stats_shape],
        query_two, cotan_two, norm_gain, stats_one, *gathered, name="forward_two",
    )
    if heads <= 4:
        others = [lax.ppermute(stats, "head", [(i, (i + d) % heads) for i in range(heads)]) for d in range(1, heads)]
        stats = sum(others, stats)
    else:
        stats = lax.psum(stats, "head")
    grad_gate, grad_up, gain_two, *parts = call(
        partial(backward_kernel, 2, norm_width, chunks, True), [hidden_f32, hidden_f32, gain_shape] + [part] * (3 * chunks),
        query_two, cotan_two, norm_gain, stats, new_weights, gate_two, up_two, out_two, name="backward_two",
    )
    arrived = scatter(parts)
    (grad_query_two,) = call(query_grad_kernel, [token_bf16], grad_gate, grad_up, new_weights, name="query_two")
    grad_gate, grad_up, gain_one, *direct_parts = call(
        partial(backward_kernel, 0, norm_width, chunks, False), [hidden_f32, hidden_f32, gain_shape] + [chunk] * chunks,
        query_one, cotan_one, norm_gain, stats, old_weights, gate_one, up_one, out_one, name="backward_one",
    )
    (grad_query_one,) = call(query_grad_kernel, [token_bf16], grad_gate, grad_up, old_weights, name="query_one")

    turn, direct, gain = call(
        renorm_back_kernel, [chunk, chunk, gain_shape], placed[-1], gain_one, gain_two, *arrived, *parts[-3:], *updates, name="renorm_back"
    )

    def back_at(step, turned, before, first=False, last=False):
        outs = [packed] + ([token_bf16, token_bf16, ((1, tokens), f32)] if last else [token_f32, token_f32])
        return call(
            partial(update_back_kernel, factor, order, step, first, last), outs, keys, values, log_rate, placed[step], turned, direct_parts[step], gain,
            *before, name="update_back",
        )

    own, *sums = back_at(chunks - 1, turn, [direct], first=True)
    total, held = None, turn
    for step in range(chunks - 1):
        held = send(held)
        mine_now, *sums = back_at(step, held, sums, last=step == chunks - 2)
        total = send(mine_now if total is None else total + mine_now)
    grad_key, grad_value, grad_rate = sums
    grad_weights, grad_gain = call(finish_kernel, [chunk, ((1, width // chunks), f32)], total, own, name="finish")
    grad_query = jnp.stack([grad_query_one, grad_query_two])[:, :, None, :]
    return grad_query, grad_key[:, None, :], grad_value[:, None, :], grad_rate, grad_weights[None], grad_gain


def solution(mesh):
    placed = (
        P(None, "ctx", "head", None),
        P("ctx", "head", None),
        P("ctx", "head", None),
        P("head", "ctx"),
        P("head", None, None, None),
        P("head", None),
        P(None, "ctx", "head", None),
    )
    return jax.shard_map(
        partial(local, mesh.shape["ctx"], mesh.shape["head"]),
        mesh=mesh,
        in_specs=placed,
        out_specs=(
            P(None, "ctx", "head", None),
            P("ctx", "head", None),
            P("ctx", "head", None),
            P("head", "ctx"),
            P("head", None, "ctx", None),
            P("head", "ctx"),
        ),
        check_vma=False,
    )
```

```python
from functools import partial

import jax
import jax.numpy as jnp
from jax import lax
from jax.experimental import pallas as pl
from jax.experimental.pallas import tpu as pltpu
from jax.sharding import PartitionSpec as P

EPSILON = 1e-06
VMEM_BYTES = 16 * 1024 * 1024
TURN_SETS, BACK_SETS = 3, 2
FIRST_VMEM, REST_VMEM = 60 * 1024 * 1024, 16 * 1024 * 1024
f32, bf16 = jnp.float32, jnp.bfloat16


def ring_order(count):
    width = max(w for w in range(1, count + 1) if count % w == 0 and w * w <= count)
    height = count // width
    if width == 1 or height % 2:
        return list(range(count))
    order = [0]
    for row in range(height):
        columns = range(1, width) if row % 2 == 0 else range(width - 1, 0, -1)
        order += [row * width + column for column in columns]
    return order + [row * width for row in range(height - 1, 0, -1)]


def ring_pairs(count, heads):
    order, pairs = ring_order(count), []
    for head in range(heads):
        way = order if head % 2 == 0 else order[::-1]
        pairs += [(way[at] * heads + head, way[(at + 1) % count] * heads + head) for at in range(count)]
    return pairs


def owner_at(order, step):
    device, sign = lax.axis_index("ctx"), 1 - 2 * lax.rem(lax.axis_index("head"), 2)
    count = len(order)
    at = sum(jnp.where(device == name, place, 0) for place, name in enumerate(order))
    place = lax.rem(at - sign * (1 + step) + 2 * count, count)
    return sum(jnp.where(place == i, name, 0) for i, name in enumerate(order))


def cuts(rows, sets):
    tiles = rows // 8
    ends = [8 * (tiles * (i + 1) // sets) for i in range(sets)]
    return list(zip([0] + ends[:-1], ends))


def pair(x):
    high = x.astype(bf16)
    return high, (x - high.astype(f32)).astype(bf16)


def nt(a, b):
    return lax.dot_general(a, b, (((1,), (1,)), ((), ())), preferred_element_type=f32)


def nn(a, b):
    return lax.dot_general(a, b, (((1,), (0,)), ((), ())), preferred_element_type=f32)


def tn(a, b):
    return lax.dot_general(a, b, (((0,), (0,)), ((), ())), preferred_element_type=f32)


def three(dot, a, b):
    (a_high, a_low), (b_high, b_low) = a, b
    return dot(a_high, b_high) + (dot(a_high, b_low) + dot(a_low, b_high))


def rows_by(x, mats):
    pairs = [pair(m) for m in mats]
    stacked = jnp.concatenate([p[0] for p in pairs] + [p[1] for p in pairs], axis=0)
    both = nt(x, stacked)
    half = both.shape[1] // 2
    total = both[:, :half] + both[:, half:]
    rows = mats[0].shape[0]
    return [total[:, i * rows : (i + 1) * rows] for i in range(len(mats))]


def sums_by(parts, x):
    pairs = [pair(m) for m in parts]
    stacked = jnp.concatenate([p[0] for p in pairs] + [p[1] for p in pairs], axis=1)
    both = tn(stacked, x)
    half = both.shape[0] // 2
    total = both[:half] + both[half:]
    rows = parts[0].shape[1]
    return [total[i * rows : (i + 1) * rows] for i in range(len(parts))]


def silu_parts(gate):
    sig = 1.0 / (1.0 + jnp.exp(-gate))
    act = gate * sig
    return sig, act, sig + act * (1.0 - sig)


def to_columns(rows):
    count, tokens = rows.shape
    if count < 128:
        rows = jnp.concatenate([rows, jnp.zeros((128 - count, tokens), f32)], axis=0)
    turned = jnp.transpose(rows)
    return [turned[:, i : i + 1] for i in range(count)]


def to_rows(columns):
    tokens = columns[0].shape[0]
    lane = lax.broadcasted_iota(jnp.int32, (tokens, 128), 1)
    packed = jnp.zeros((tokens, 128), f32)
    for i, column in enumerate(columns):
        packed = jnp.where(lane == i, column, packed)
    return jnp.transpose(packed)[:8]


def minus_rate(rate_ref, factor):
    return -jnp.exp(to_columns(rate_ref[...])[0]) * factor


def write_parts(parts_ref, sums, steps):
    rows = sums[0].shape[0] // steps
    for step in range(steps):
        for i, total in enumerate(sums):
            parts_ref[3 * step + i][...] = total[step * rows : (step + 1) * rows]


def update_kernel(factor, order, first, steps, weights_ref, key_ref, value_ref, rate_ref, *refs):
    placed_ref, key_here, value_here, weight_sems, token_sems = refs[-5:]
    parts_ref, chunks_ref = refs[: 3 * steps], refs[3 * steps : -5]
    rows = weights_ref.shape[1] // len(order)
    copies = [pltpu.make_async_copy(key_ref, key_here, token_sems.at[0])]
    copies[0].start()
    for step in range(steps):
        source = weights_ref.at[:, pl.ds(pl.multiple_of(owner_at(order, first + step) * rows, rows), rows), :]
        copy = pltpu.make_async_copy(source, placed_ref.at[:, pl.ds(step * rows, rows), :], weight_sems.at[step])
        copy.start()
        copies.append(copy)
    copy = pltpu.make_async_copy(value_ref, value_here, token_sems.at[1])
    copy.start()
    rate = minus_rate(rate_ref, factor)
    for copy in copies + [copy]:
        copy.wait()
    keys, values = key_here[...], value_here[...]
    gate, up = rows_by(keys, [placed_ref[0], placed_ref[1]])
    (back,) = rows_by(values, [placed_ref[2]])
    _, act, slope = silu_parts(gate)
    back = back * rate
    grad_gate, grad_up = sums_by([back * up * slope, back * act], keys)
    (grad_down,) = sums_by([act * up * rate], values)
    write_parts(parts_ref, [grad_gate, grad_up, grad_down], steps)
    for step, chunk_ref in enumerate(chunks_ref):
        chunk_ref[...] = placed_ref[:, step * rows : (step + 1) * rows, :]


def scales(update, anchor):
    target = jnp.sqrt(jnp.sum(anchor * anchor, axis=-1, keepdims=True) + EPSILON)
    actual = jnp.sqrt(jnp.sum(update * update, axis=-1, keepdims=True) + EPSILON)
    return target, actual


def renorm_kernel(which, arrived_ref, mine_ref, anchor_ref, update_ref, new_ref):
    anchor = anchor_ref[which]
    update = anchor - (arrived_ref[...] + mine_ref[...])
    target, actual = scales(update, anchor)
    update_ref[...] = update
    new_ref[...] = update * (target / actual)


def renorm_back_kernel(which, arrived_ref, mine_ref, update_ref, anchor_ref, turned_ref, direct_ref):
    anchor, update, cot = anchor_ref[which], update_ref[...], arrived_ref[...] + mine_ref[...]
    target, actual = scales(update, anchor)
    inner = jnp.sum(update * cot, axis=-1, keepdims=True)
    ratio = target / actual
    update_cot = ratio * cot - update * (inner * ratio / (actual * actual))
    turned_ref[...] = -update_cot
    direct_ref[...] = update_cot + anchor * (inner / (actual * target))


def forward_pass(queries, gate_mat, up_mat, down_mat):
    gate, up = rows_by(queries, [gate_mat, up_mat])
    _, act, _ = silu_parts(gate)
    out = three(nn, pair(act * up), pair(down_mat))
    return gate, up, out


def norm_sums(out, cotan, gain):
    return [jnp.sum(out * out, axis=1, keepdims=True), jnp.sum(gain * cotan * out, axis=1, keepdims=True)]


def forward_kernel(count, other, query_ref, cotan_ref, gain_ref, *refs):
    if other:
        other_ref, refs = refs[0], refs[1:]
    chunks, (weights_ref, gate_ref, up_ref, out_ref, stats_ref) = refs[:count], refs[count:]
    rows = weights_ref.shape[1] // (count if len(chunks[0].shape) == 3 else count // 3)
    for i, chunk in enumerate(chunks):
        if len(chunk.shape) == 3:
            weights_ref[:, i * rows : (i + 1) * rows, :] = chunk[...]
        else:
            weights_ref[i % 3, i // 3 * rows : (i // 3 + 1) * rows, :] = chunk[...]
    gate, up, out = forward_pass(query_ref[...], weights_ref[0], weights_ref[1], weights_ref[2])
    gate_ref[...] = gate
    up_ref[...] = up
    out_ref[...] = out
    sums = norm_sums(out, cotan_ref[...].astype(f32), gain_ref[...])
    if other:
        stats_ref[...] = to_rows([jnp.zeros((out.shape[0], 1), f32)] * 2 + sums) + other_ref[...]
    else:
        stats_ref[...] = to_rows(sums)


def backward_kernel(first, width, chunks, split, query_ref, cotan_ref, gain_ref, stats_ref, weights_ref, gate_ref, up_ref, out_ref, grad_gate_ref, grad_up_ref, gain_term_ref, *parts_ref):
    columns = to_columns(stats_ref[...])
    square, product = columns[first], columns[first + 1]
    inverse = 1.0 / jnp.sqrt(square / width + EPSILON)
    out, cotan = out_ref[...], cotan_ref[...].astype(f32)
    grad_out = gain_ref[...] * cotan * inverse - out * (inverse * inverse * inverse * product / width)
    gain_term_ref[...] = jnp.sum(cotan * out * inverse, axis=0, keepdims=True)
    up = up_ref[...]
    _, act, slope = silu_parts(gate_ref[...])
    grad_out = pair(grad_out)
    back = three(nt, grad_out, pair(weights_ref[2]))
    grad_gate, grad_up = back * up * slope, back * act
    grad_gate_ref[...] = grad_gate
    grad_up_ref[...] = grad_up
    sum_gate, sum_up = sums_by([grad_gate, grad_up], query_ref[...])
    sum_down = three(tn, pair(act * up), grad_out)
    if split:
        write_parts(parts_ref, [sum_gate, sum_up, sum_down], chunks)
    else:
        rows = sum_gate.shape[0] // chunks
        for step in range(chunks):
            for i, total in enumerate((sum_gate, sum_up, sum_down)):
                parts_ref[step][i] = total[step * rows : (step + 1) * rows]


def query_grad_kernel(grad_gate_ref, grad_up_ref, weights_ref, out_ref):
    total = three(nn, pair(grad_gate_ref[...]), pair(weights_ref[0]))
    total = total + three(nn, pair(grad_up_ref[...]), pair(weights_ref[1]))
    out_ref[...] = total.astype(bf16)


def second_order(keys, values, rate, weights, turns):
    gate, up, gate_turn, up_turn = rows_by(keys, [weights[0], weights[1], turns[0], turns[1]])
    back, back_turn = rows_by(values, [weights[2], turns[2]])
    back, back_turn = back * rate, back_turn * rate
    sig, act, slope = silu_parts(gate)
    bend = sig * (1.0 - sig) * (2.0 + gate * (1.0 - 2.0 * sig))
    hidden_turn = slope * gate_turn * up + act * up_turn
    cot_gate = back * (bend * gate_turn * up + slope * up_turn) + back_turn * up * slope
    cot_up = back * slope * gate_turn + back_turn * act
    return act * up, hidden_turn, cot_gate, cot_up, back * slope * up, back * act


def update_back_kernel(factor, order, step, first, last, key_ref, value_ref, rate_ref, weights_ref, gathered_ref, gain_one_ref, gain_two_ref, *refs):
    turns_ref, refs = refs[:3], refs[3:]
    if first:
        direct_ref, refs = refs[:3], refs[3:]
    else:
        before_key_ref, before_value_ref, refs = refs[0], refs[1], refs[2:]
    outs_ref, (grad_key_ref, grad_value_ref), refs = refs[:BACK_SETS], refs[BACK_SETS : BACK_SETS + 2], refs[BACK_SETS + 2 :]
    keys, values = key_ref[...], value_ref[...]
    rate = minus_rate(rate_ref, factor)
    weights, turns = [weights_ref[i] for i in range(3)], [t[...] for t in turns_ref]
    hidden, hidden_turn, cot_gate, cot_up, cot_gate_turn, cot_up_turn = second_order(keys, values, rate, weights, turns)
    sums = sums_by([cot_gate, cot_up], keys) + sums_by([hidden_turn * rate], values)
    sums = [total + gathered_ref[i] for i, total in enumerate(sums)]
    if first:
        sums = [total + direct_ref[i][...] for i, total in enumerate(sums)]
    gain = jnp.broadcast_to(gain_one_ref[...] + gain_two_ref[...], (8, gain_one_ref.shape[1]))
    piece = gain.shape[1] // len(order)
    sums.append(pltpu.roll(gain, lax.rem((len(order) - owner_at(order, step)) * piece, gain.shape[1]), 1))
    packed, at = jnp.concatenate(sums, axis=0), 0
    for out_ref in outs_ref:
        out_ref[...] = packed[at : at + out_ref.shape[0]]
        at += out_ref.shape[0]
    grad_key = three(nn, pair(jnp.concatenate([cot_gate, cot_up, cot_gate_turn, cot_up_turn], axis=1)), pair(jnp.concatenate([weights[0], weights[1], turns[0], turns[1]], axis=0)))
    grad_value = rate * three(nn, pair(jnp.concatenate([hidden_turn, hidden], axis=1)), pair(jnp.concatenate([weights[2], turns[2]], axis=0)))
    if not first:
        grad_key, grad_value = grad_key + before_key_ref[...], grad_value + before_value_ref[...]
    grad_key_ref[...] = grad_key.astype(grad_key_ref.dtype)
    grad_value_ref[...] = grad_value.astype(grad_value_ref.dtype)
    if last:
        refs[0][...] = to_rows([jnp.sum(grad_value * values.astype(f32), axis=1, keepdims=True)])[:1]


def finish_kernel(*refs):
    arrived, mine, (weights_ref, gain_ref) = refs[:BACK_SETS], refs[BACK_SETS : 2 * BACK_SETS], refs[2 * BACK_SETS :]
    rows = weights_ref.shape[1]
    total = jnp.concatenate([a[...] + m[...] for a, m in zip(arrived, mine)], axis=0)
    for i in range(3):
        weights_ref[i] = total[i * rows : (i + 1) * rows]
    gain_ref[...] = total[3 * rows : 3 * rows + 1, : gain_ref.shape[1]]


def call(kernel, outs, *args, in_hbm=0, scratch=(), name=None, micros=4, vmem=VMEM_BYTES):
    in_specs = [pl.BlockSpec(memory_space=pl.ANY)] * in_hbm + [pl.BlockSpec(memory_space=pltpu.VMEM)] * (len(args) - in_hbm)
    return pl.pallas_call(
        kernel,
        out_shape=[jax.ShapeDtypeStruct(shape, dtype) for shape, dtype in outs],
        in_specs=in_specs,
        out_specs=[pl.BlockSpec(memory_space=pltpu.VMEM)] * len(outs),
        scratch_shapes=scratch,
        compiler_params=pltpu.CompilerParams(vmem_limit_bytes=vmem),
        cost_estimate=pl.CostEstimate(flops=int(micros * 1e9), transcendentals=0, bytes_accessed=int(micros * 3e6)),
        name=name,
    )(*args)


def local(chunks, heads, query_tokens, key_tokens, value_tokens, log_rate, fast_weights, norm_gain, out_grad):
    order, pairs = ring_order(chunks), ring_pairs(chunks, heads)

    def send(x):
        return lax.ppermute(x, ("ctx", "head"), pairs)

    weights = fast_weights[0]
    query_one, query_two = query_tokens[0, :, 0, :], query_tokens[1, :, 0, :]
    cotan_one, cotan_two = out_grad[0, :, 0, :], out_grad[1, :, 0, :]
    keys, values = key_tokens[:, 0, :], value_tokens[:, 0, :]
    tokens, width = keys.shape
    hidden = weights.shape[1]
    rows = hidden // chunks
    factor = (tokens * chunks * width) ** (-0.5)
    norm_width = heads * width
    token_f32, token_bf16, whole = ((tokens, width), f32), ((tokens, width), bf16), ((3, hidden, width), f32)
    hidden_f32, stats_shape, gain_shape = ((tokens, hidden), f32), ((8, tokens), f32), ((1, width), f32)
    chunk, part = ((3, rows, width), f32), ((rows, width), f32)

    def scatter(parts):
        totals = list(parts[:3])
        for step in range(chunks - 1):
            totals = [send(t) for t in totals]
            if step < chunks - 2:
                totals = [t + p for t, p in zip(totals, parts[3 * step + 3 :])]
        return totals

    def update(first, steps, keep, vmem):
        return call(
            partial(update_kernel, factor, order, first, steps), [part] * (3 * steps) + ([chunk] * steps if keep else []), weights, keys, values, log_rate,
            in_hbm=3, vmem=vmem, name="update",
            scratch=[pltpu.VMEM((3, steps * rows, width), f32), pltpu.VMEM((tokens, width), bf16), pltpu.VMEM((tokens, width), bf16)]
            + [pltpu.SemaphoreType.DMA((steps,)), pltpu.SemaphoreType.DMA((2,))],
        )

    parts = update(0, 1, True, FIRST_VMEM)
    parts, placed = parts[:3], parts[3:]
    rest = update(1, chunks - 1, True, REST_VMEM)
    parts, placed = parts + rest[: -(chunks - 1)], placed + rest[-(chunks - 1) :]
    arrived = scatter(parts)
    old_weights, gate_one, up_one, out_one, stats_one = call(
        partial(forward_kernel, chunks, False), [whole, hidden_f32, hidden_f32, token_f32, stats_shape], query_one, cotan_one, norm_gain, *placed, name="forward_one"
    )
    updates, gathered = [], []
    for i in range(3):
        new = call(partial(renorm_kernel, i), [part] * 2, arrived[i], parts[i - 3], placed[-1], name="renorm")
        updates.append(new[0])
        gathered.append(new[1])
    held, gathered = gathered, []
    news = held
    for step in range(chunks - 1):
        held = [send(h) for h in held]
        gathered += held
    gathered += news

    new_weights, gate_two, up_two, out_two, stats = call(
        partial(forward_kernel, len(gathered), True), [whole, hidden_f32, hidden_f32, token_f32, stats_shape],
        query_two, cotan_two, norm_gain, stats_one, *gathered, name="forward_two",
    )
    if heads <= 4:
        others = [lax.ppermute(stats, "head", [(i, (i + d) % heads) for i in range(heads)]) for d in range(1, heads)]
        stats = sum(others, stats)
    else:
        stats = lax.psum(stats, "head")
    grad_gate, grad_up, gain_two, *parts = call(
        partial(backward_kernel, 2, norm_width, chunks, True), [hidden_f32, hidden_f32, gain_shape] + [part] * (3 * chunks),
        query_two, cotan_two, norm_gain, stats, new_weights, gate_two, up_two, out_two, name="backward_two",
    )
    arrived = scatter(parts)
    (grad_query_two,) = call(query_grad_kernel, [token_bf16], grad_gate, grad_up, new_weights, name="query_two")
    grad_gate, grad_up, gain_one, *direct_parts = call(
        partial(backward_kernel, 0, norm_width, chunks, False), [hidden_f32, hidden_f32, gain_shape] + [chunk] * chunks,
        query_one, cotan_one, norm_gain, stats, old_weights, gate_one, up_one, out_one, name="backward_one",
    )
    (grad_query_one,) = call(query_grad_kernel, [token_bf16], grad_gate, grad_up, old_weights, name="query_one")

    turned = [
        call(partial(renorm_back_kernel, i), [part] * 2, arrived[i], parts[i - 3], updates[i], placed[-1], name="renorm_back") for i in range(3)
    ]
    turn, direct = [t[0] for t in turned], [t[1] for t in turned]
    packed = [((end - start, width), f32) for start, end in cuts(3 * rows + 8, BACK_SETS)]

    def back_at(step, turned, before, first=False, last=False):
        outs = packed + ([token_bf16, token_bf16, ((1, tokens), f32)] if last else [token_f32, token_f32])
        outs = call(
            partial(update_back_kernel, factor, order, step, first, last), outs, keys, values, log_rate, placed[step], direct_parts[step], gain_one, gain_two,
            *turned, *before, name="update_back",
        )
        return outs[:BACK_SETS], outs[BACK_SETS:]

    own, sums = back_at(chunks - 1, turn, direct, first=True)
    totals, held = None, turn if TURN_SETS == 3 else jnp.concatenate([t[None] for t in turn])
    for step in range(chunks - 1):
        if TURN_SETS == 3:
            held = [send(h) for h in held]
        else:
            held = send(held)
        mine_now, sums = back_at(step, held if TURN_SETS == 3 else [held[i] for i in range(3)], sums, last=step == chunks - 2)
        totals = [send(m if totals is None else totals[i] + m) for i, m in enumerate(mine_now)]
    grad_key, grad_value, grad_rate = sums
    grad_weights, grad_gain = call(finish_kernel, [chunk, ((1, width // chunks), f32)], *totals, *own, name="finish")
    grad_query = jnp.stack([grad_query_one, grad_query_two])[:, :, None, :]
    return grad_query, grad_key[:, None, :], grad_value[:, None, :], grad_rate, grad_weights[None], grad_gain


def solution(mesh):
    placed = (
        P(None, "ctx", "head", None),
        P("ctx", "head", None),
        P("ctx", "head", None),
        P("head", "ctx"),
        P("head", None, None, None),
        P("head", None),
        P(None, "ctx", "head", None),
    )
    return jax.shard_map(
        partial(local, mesh.shape["ctx"], mesh.shape["head"]),
        mesh=mesh,
        in_specs=placed,
        out_specs=(
            P(None, "ctx", "head", None),
            P("ctx", "head", None),
            P("ctx", "head", None),
            P("head", "ctx"),
            P("head", None, "ctx", None),
            P("head", "ctx"),
        ),
        check_vma=False,
    )
```

```python
from functools import partial

import jax
import jax.numpy as jnp
from jax import lax
from jax.experimental import pallas as pl
from jax.experimental.pallas import tpu as pltpu
from jax.sharding import PartitionSpec as P

EPSILON = 1e-06
VMEM_BYTES = 16 * 1024 * 1024
SETS, TURN_SETS, BACK_SETS = 4, 2, 2
FIRST_VMEM, REST_VMEM = 60 * 1024 * 1024, 16 * 1024 * 1024
f32, bf16 = jnp.float32, jnp.bfloat16


def ring_order(count):
    width = max(w for w in range(1, count + 1) if count % w == 0 and w * w <= count)
    height = count // width
    if width == 1 or height % 2:
        return list(range(count))
    order = [0]
    for row in range(height):
        columns = range(1, width) if row % 2 == 0 else range(width - 1, 0, -1)
        order += [row * width + column for column in columns]
    return order + [row * width for row in range(height - 1, 0, -1)]


def ring_pairs(count, heads):
    order, pairs = ring_order(count), []
    for head in range(heads):
        way = order if head % 2 == 0 else order[::-1]
        pairs += [(way[at] * heads + head, way[(at + 1) % count] * heads + head) for at in range(count)]
    return pairs


def owner_at(order, step):
    device, sign = lax.axis_index("ctx"), 1 - 2 * lax.rem(lax.axis_index("head"), 2)
    count = len(order)
    at = sum(jnp.where(device == name, place, 0) for place, name in enumerate(order))
    place = lax.rem(at - sign * (1 + step) + 2 * count, count)
    return sum(jnp.where(place == i, name, 0) for i, name in enumerate(order))


def cuts(rows, sets):
    tiles = rows // 8
    ends = [8 * (tiles * (i + 1) // sets) for i in range(sets)]
    return list(zip([0] + ends[:-1], ends))


def pair(x):
    high = x.astype(bf16)
    return high, (x - high.astype(f32)).astype(bf16)


def nt(a, b):
    return lax.dot_general(a, b, (((1,), (1,)), ((), ())), preferred_element_type=f32)


def nn(a, b):
    return lax.dot_general(a, b, (((1,), (0,)), ((), ())), preferred_element_type=f32)


def tn(a, b):
    return lax.dot_general(a, b, (((0,), (0,)), ((), ())), preferred_element_type=f32)


def three(dot, a, b):
    (a_high, a_low), (b_high, b_low) = a, b
    return dot(a_high, b_high) + (dot(a_high, b_low) + dot(a_low, b_high))


def rows_by(x, mats):
    pairs = [pair(m) for m in mats]
    stacked = jnp.concatenate([p[0] for p in pairs] + [p[1] for p in pairs], axis=0)
    both = nt(x, stacked)
    half = both.shape[1] // 2
    total = both[:, :half] + both[:, half:]
    rows = mats[0].shape[0]
    return [total[:, i * rows : (i + 1) * rows] for i in range(len(mats))]


def sums_by(parts, x):
    pairs = [pair(m) for m in parts]
    stacked = jnp.concatenate([p[0] for p in pairs] + [p[1] for p in pairs], axis=1)
    both = tn(stacked, x)
    half = both.shape[0] // 2
    total = both[:half] + both[half:]
    rows = parts[0].shape[1]
    return [total[i * rows : (i + 1) * rows] for i in range(len(parts))]


def silu_parts(gate):
    sig = 1.0 / (1.0 + jnp.exp(-gate))
    act = gate * sig
    return sig, act, sig + act * (1.0 - sig)


def to_columns(rows):
    count, tokens = rows.shape
    if count < 128:
        rows = jnp.concatenate([rows, jnp.zeros((128 - count, tokens), f32)], axis=0)
    turned = jnp.transpose(rows)
    return [turned[:, i : i + 1] for i in range(count)]


def to_rows(columns):
    tokens = columns[0].shape[0]
    lane = lax.broadcasted_iota(jnp.int32, (tokens, 128), 1)
    packed = jnp.zeros((tokens, 128), f32)
    for i, column in enumerate(columns):
        packed = jnp.where(lane == i, column, packed)
    return jnp.transpose(packed)[:8]


def minus_rate(rate_ref, factor):
    return -jnp.exp(to_columns(rate_ref[...])[0]) * factor


def write_parts(parts_ref, sums, steps):
    piece = sums[0].shape[0] // steps // SETS
    for at, part_ref in enumerate(parts_ref):
        for i, total in enumerate(sums):
            part_ref[i] = total[at * piece : (at + 1) * piece]


def update_kernel(factor, order, first, steps, weights_ref, key_ref, value_ref, rate_ref, *refs):
    placed_ref, key_here, value_here, weight_sems, token_sems = refs[-5:]
    parts_ref, chunks_ref = refs[: SETS * steps], refs[SETS * steps : -5]
    rows = weights_ref.shape[1] // len(order)
    copies = [pltpu.make_async_copy(key_ref, key_here, token_sems.at[0])]
    copies[0].start()
    for step in range(steps):
        source = weights_ref.at[:, pl.ds(pl.multiple_of(owner_at(order, first + step) * rows, rows), rows), :]
        copy = pltpu.make_async_copy(source, placed_ref.at[:, pl.ds(step * rows, rows), :], weight_sems.at[step])
        copy.start()
        copies.append(copy)
    copy = pltpu.make_async_copy(value_ref, value_here, token_sems.at[1])
    copy.start()
    rate = minus_rate(rate_ref, factor)
    for copy in copies + [copy]:
        copy.wait()
    keys, values = key_here[...], value_here[...]
    gate, up = rows_by(keys, [placed_ref[0], placed_ref[1]])
    (back,) = rows_by(values, [placed_ref[2]])
    _, act, slope = silu_parts(gate)
    back = back * rate
    grad_gate, grad_up = sums_by([back * up * slope, back * act], keys)
    (grad_down,) = sums_by([act * up * rate], values)
    write_parts(parts_ref, [grad_gate, grad_up, grad_down], steps)
    for step, chunk_ref in enumerate(chunks_ref):
        chunk_ref[...] = placed_ref[:, step * rows : (step + 1) * rows, :]


def scales(update, anchor):
    target = jnp.sqrt(jnp.sum(anchor * anchor, axis=-1, keepdims=True) + EPSILON)
    actual = jnp.sqrt(jnp.sum(update * update, axis=-1, keepdims=True) + EPSILON)
    return target, actual


def renorm_kernel(start, arrived_ref, mine_ref, anchor_ref, update_ref, new_ref):
    anchor = anchor_ref[:, start : start + update_ref.shape[1], :]
    update = anchor - (arrived_ref[...] + mine_ref[...])
    target, actual = scales(update, anchor)
    update_ref[...] = update
    new_ref[...] = update * (target / actual)


def renorm_back_kernel(start, anchor_ref, *refs):
    sets, (turned_ref, direct_ref) = (len(refs) - 2) // 3, refs[-2:]
    piece = refs[0].shape[1]
    for i in range(sets):
        at = slice(i * piece, (i + 1) * piece)
        anchor = anchor_ref[:, start + i * piece : start + (i + 1) * piece, :]
        cot, update = refs[i][...] + refs[sets + i][...], refs[2 * sets + i][...]
        target, actual = scales(update, anchor)
        inner = jnp.sum(update * cot, axis=-1, keepdims=True)
        ratio = target / actual
        update_cot = ratio * cot - update * (inner * ratio / (actual * actual))
        turned_ref[:, at, :] = -update_cot
        direct_ref[:, at, :] = update_cot + anchor * (inner / (actual * target))


def forward_pass(queries, gate_mat, up_mat, down_mat):
    gate, up = rows_by(queries, [gate_mat, up_mat])
    _, act, _ = silu_parts(gate)
    out = three(nn, pair(act * up), pair(down_mat))
    return gate, up, out


def norm_sums(out, cotan, gain):
    return [jnp.sum(out * out, axis=1, keepdims=True), jnp.sum(gain * cotan * out, axis=1, keepdims=True)]


def forward_kernel(count, other, query_ref, cotan_ref, gain_ref, *refs):
    if other:
        other_ref, refs = refs[0], refs[1:]
    chunks, (weights_ref, gate_ref, up_ref, out_ref, stats_ref) = refs[:count], refs[count:]
    rows = weights_ref.shape[1] // count
    for i, chunk in enumerate(chunks):
        weights_ref[:, i * rows : (i + 1) * rows, :] = chunk[...]
    gate, up, out = forward_pass(query_ref[...], weights_ref[0], weights_ref[1], weights_ref[2])
    gate_ref[...] = gate
    up_ref[...] = up
    out_ref[...] = out
    sums = norm_sums(out, cotan_ref[...].astype(f32), gain_ref[...])
    if other:
        stats_ref[...] = to_rows([jnp.zeros((out.shape[0], 1), f32)] * 2 + sums) + other_ref[...]
    else:
        stats_ref[...] = to_rows(sums)


def out_cotangent(first, width, cotan_ref, gain_ref, stats_ref, out_ref):
    columns = to_columns(stats_ref[...])
    square, product = columns[first], columns[first + 1]
    inverse = 1.0 / jnp.sqrt(square / width + EPSILON)
    out, cotan = out_ref[...], cotan_ref[...].astype(f32)
    grad_out = gain_ref[...] * cotan * inverse - out * (inverse * inverse * inverse * product / width)
    return pair(grad_out), jnp.sum(cotan * out * inverse, axis=0, keepdims=True)


def backward_sums(queries, grad_out, gate, up, down_mat):
    _, act, slope = silu_parts(gate)
    back = three(nt, grad_out, pair(down_mat))
    grad_gate, grad_up = back * up * slope, back * act
    return grad_gate, grad_up, sums_by([grad_gate, grad_up], queries) + [three(tn, pair(act * up), grad_out)]


def backward_first_kernel(first, width, query_ref, cotan_ref, gain_ref, stats_ref, weights_ref, gate_ref, up_ref, out_ref, *parts_ref):
    grad_out, _ = out_cotangent(first, width, cotan_ref, gain_ref, stats_ref, out_ref)
    at = slice(0, SETS * parts_ref[0].shape[1])
    _, _, sums = backward_sums(query_ref[...], grad_out, gate_ref[:, at], up_ref[:, at], weights_ref[2, at])
    write_parts(parts_ref, sums, 1)


def backward_kernel(first, width, chunks, split, query_ref, cotan_ref, gain_ref, stats_ref, weights_ref, gate_ref, up_ref, out_ref, grad_gate_ref, grad_up_ref, gain_term_ref, *parts_ref):
    grad_out, gain_term_ref[...] = out_cotangent(first, width, cotan_ref, gain_ref, stats_ref, out_ref)
    grad_gate_ref[...], grad_up_ref[...], sums = backward_sums(query_ref[...], grad_out, gate_ref[...], up_ref[...], weights_ref[2])
    rows = sums[0].shape[0] // chunks
    if split:
        write_parts(parts_ref, [total[rows:] for total in sums], chunks - 1)
    else:
        for step in range(chunks):
            for i, total in enumerate(sums):
                parts_ref[step][i] = total[step * rows : (step + 1) * rows]


def token_kernel(key_sum_ref, value_sum_ref, value_ref, *refs):
    blocks, (grad_query_ref, grad_key_ref, grad_value_ref, grad_rate_ref) = refs[:-4], refs[-4:]
    grad_value = value_sum_ref[...]
    grad_rate_ref[...] = to_rows([jnp.sum(grad_value * value_ref[...].astype(f32), axis=1, keepdims=True)])[:1]
    grad_key_ref[...] = key_sum_ref[...].astype(bf16)
    grad_value_ref[...] = grad_value.astype(bf16)
    for block in range(2):
        grad_gate_ref, grad_up_ref, weights_ref = blocks[3 * block : 3 * block + 3]
        total = three(nn, pair(grad_gate_ref[...]), pair(weights_ref[0]))
        total = total + three(nn, pair(grad_up_ref[...]), pair(weights_ref[1]))
        grad_query_ref[block] = total.astype(bf16)


def second_order(keys, values, rate, weights, turns):
    gate, up, gate_turn, up_turn = rows_by(keys, [weights[0], weights[1], turns[0], turns[1]])
    back, back_turn = rows_by(values, [weights[2], turns[2]])
    back, back_turn = back * rate, back_turn * rate
    sig, act, slope = silu_parts(gate)
    bend = sig * (1.0 - sig) * (2.0 + gate * (1.0 - 2.0 * sig))
    hidden_turn = slope * gate_turn * up + act * up_turn
    cot_gate = back * (bend * gate_turn * up + slope * up_turn) + back_turn * up * slope
    cot_up = back * slope * gate_turn + back_turn * act
    return act * up, hidden_turn, cot_gate, cot_up, back * slope * up, back * act


def update_back_kernel(factor, order, step, first, key_ref, value_ref, rate_ref, weights_ref, gathered_ref, gain_one_ref, gain_two_ref, *refs):
    turns_ref, refs = refs[:TURN_SETS], refs[TURN_SETS:]
    if first:
        direct_ref, refs = refs[:TURN_SETS], refs[TURN_SETS:]
    else:
        before_key_ref, before_value_ref, refs = refs[0], refs[1], refs[2:]
    outs_ref, (grad_key_ref, grad_value_ref) = refs[:BACK_SETS], refs[BACK_SETS:]
    keys, values = key_ref[...], value_ref[...]
    rate = minus_rate(rate_ref, factor)
    weights, turns = [weights_ref[i] for i in range(3)], [jnp.concatenate([t[i] for t in turns_ref], axis=0) for i in range(3)]
    hidden, hidden_turn, cot_gate, cot_up, cot_gate_turn, cot_up_turn = second_order(keys, values, rate, weights, turns)
    sums = sums_by([cot_gate, cot_up], keys) + sums_by([hidden_turn * rate], values)
    sums = [total + gathered_ref[i] for i, total in enumerate(sums)]
    if first:
        sums = [total + jnp.concatenate([d[i] for d in direct_ref], axis=0) for i, total in enumerate(sums)]
    gain = jnp.broadcast_to(gain_one_ref[...] + gain_two_ref[...], (8, gain_one_ref.shape[1]))
    piece = gain.shape[1] // len(order)
    sums.append(pltpu.roll(gain, lax.rem((len(order) - owner_at(order, step)) * piece, gain.shape[1]), 1))
    packed, at = jnp.concatenate(sums, axis=0), 0
    for out_ref in outs_ref:
        out_ref[...] = packed[at : at + out_ref.shape[0]]
        at += out_ref.shape[0]
    grad_key = three(nn, pair(jnp.concatenate([cot_gate, cot_up, cot_gate_turn, cot_up_turn], axis=1)), pair(jnp.concatenate([weights[0], weights[1], turns[0], turns[1]], axis=0)))
    grad_value = rate * three(nn, pair(jnp.concatenate([hidden_turn, hidden], axis=1)), pair(jnp.concatenate([weights[2], turns[2]], axis=0)))
    if not first:
        grad_key, grad_value = grad_key + before_key_ref[...], grad_value + before_value_ref[...]
    grad_key_ref[...] = grad_key
    grad_value_ref[...] = grad_value


def finish_kernel(*refs):
    arrived, mine, (weights_ref, gain_ref) = refs[:BACK_SETS], refs[BACK_SETS : 2 * BACK_SETS], refs[2 * BACK_SETS :]
    rows = weights_ref.shape[1]
    total = jnp.concatenate([a[...] + m[...] for a, m in zip(arrived, mine)], axis=0)
    for i in range(3):
        weights_ref[i] = total[i * rows : (i + 1) * rows]
    gain_ref[...] = total[3 * rows : 3 * rows + 1, : gain_ref.shape[1]]


def call(kernel, outs, *args, in_hbm=0, scratch=(), name=None, micros=4, vmem=VMEM_BYTES):
    in_specs = [pl.BlockSpec(memory_space=pl.ANY)] * in_hbm + [pl.BlockSpec(memory_space=pltpu.VMEM)] * (len(args) - in_hbm)
    return pl.pallas_call(
        kernel,
        out_shape=[jax.ShapeDtypeStruct(shape, dtype) for shape, dtype in outs],
        in_specs=in_specs,
        out_specs=[pl.BlockSpec(memory_space=pltpu.VMEM)] * len(outs),
        scratch_shapes=scratch,
        compiler_params=pltpu.CompilerParams(vmem_limit_bytes=vmem),
        cost_estimate=pl.CostEstimate(flops=int(micros * 1e9), transcendentals=0, bytes_accessed=int(micros * 3e6)),
        name=name,
    )(*args)


def local(chunks, heads, query_tokens, key_tokens, value_tokens, log_rate, fast_weights, norm_gain, out_grad):
    order, pairs = ring_order(chunks), ring_pairs(chunks, heads)

    def send(x):
        return lax.ppermute(x, ("ctx", "head"), pairs)

    weights = fast_weights[0]
    query_one, query_two = query_tokens[0, :, 0, :], query_tokens[1, :, 0, :]
    cotan_one, cotan_two = out_grad[0, :, 0, :], out_grad[1, :, 0, :]
    keys, values = key_tokens[:, 0, :], value_tokens[:, 0, :]
    tokens, width = keys.shape
    hidden = weights.shape[1]
    rows = hidden // chunks
    factor = (tokens * chunks * width) ** (-0.5)
    norm_width = heads * width
    token_f32, token_bf16, whole = ((tokens, width), f32), ((tokens, width), bf16), ((3, hidden, width), f32)
    hidden_f32, stats_shape, gain_shape = ((tokens, hidden), f32), ((8, tokens), f32), ((1, width), f32)
    piece = rows // SETS
    chunk, part, turn_part = ((3, rows, width), f32), ((3, piece, width), f32), ((3, rows // TURN_SETS, width), f32)

    def scatter(parts):
        totals = list(parts[:SETS])
        for step in range(chunks - 1):
            totals = [send(t) for t in totals]
            if step < chunks - 2:
                totals = [t + p for t, p in zip(totals, parts[SETS * (step + 1) :])]
        return totals

    def update(first, steps, keep, vmem):
        return call(
            partial(update_kernel, factor, order, first, steps), [part] * (SETS * steps) + ([chunk] * steps if keep else []), weights, keys, values, log_rate,
            in_hbm=3, vmem=vmem, name="update",
            scratch=[pltpu.VMEM((3, steps * rows, width), f32), pltpu.VMEM((tokens, width), bf16), pltpu.VMEM((tokens, width), bf16)]
            + [pltpu.SemaphoreType.DMA((steps,)), pltpu.SemaphoreType.DMA((2,))],
        )

    parts = update(0, 1, True, FIRST_VMEM)
    parts, placed = parts[:SETS], parts[SETS:]
    rest = update(1, chunks - 1, True, REST_VMEM)
    parts, placed = parts + rest[: -(chunks - 1)], placed + rest[-(chunks - 1) :]
    arrived = scatter(parts)
    old_weights, gate_one, up_one, out_one, stats_one = call(
        partial(forward_kernel, chunks, False), [whole, hidden_f32, hidden_f32, token_f32, stats_shape], query_one, cotan_one, norm_gain, *placed, name="forward_one"
    )
    updates, gathered = [], []
    for i in range(SETS):
        new = call(partial(renorm_kernel, i * piece), [part] * 2, arrived[i], parts[i - SETS], placed[-1], name="renorm")
        updates.append(new[0])
        gathered.append(new[1])
    held, gathered = gathered, []
    news = held
    for step in range(chunks - 1):
        held = [send(h) for h in held]
        gathered += held
    gathered += news

    new_weights, gate_two, up_two, out_two, stats = call(
        partial(forward_kernel, len(gathered), True), [whole, hidden_f32, hidden_f32, token_f32, stats_shape],
        query_two, cotan_two, norm_gain, stats_one, *gathered, name="forward_two",
    )
    if heads <= 4:
        others = [lax.ppermute(stats, "head", [(i, (i + d) % heads) for i in range(heads)]) for d in range(1, heads)]
        stats = sum(others, stats)
    else:
        stats = lax.psum(stats, "head")
    cotangent = query_two, cotan_two, norm_gain, stats
    parts = call(
        partial(backward_first_kernel, 2, norm_width), [part] * SETS, *cotangent, new_weights, gate_two, up_two, out_two, name="backward_two_first"
    )
    grad_gate_two, grad_up_two, gain_two, *rest = call(
        partial(backward_kernel, 2, norm_width, chunks, True), [hidden_f32, hidden_f32, gain_shape] + [part] * (SETS * (chunks - 1)),
        *cotangent, new_weights, gate_two, up_two, out_two, name="backward_two",
    )
    parts = [*parts, *rest]
    arrived = scatter(parts)
    grad_gate_one, grad_up_one, gain_one, *direct_parts = call(
        partial(backward_kernel, 0, norm_width, chunks, False), [hidden_f32, hidden_f32, gain_shape] + [chunk] * chunks,
        query_one, cotan_one, norm_gain, stats, old_weights, gate_one, up_one, out_one, name="backward_one",
    )

    own, turned, each = parts[-SETS:], [], SETS // TURN_SETS
    for i in range(TURN_SETS):
        at = slice(i * each, (i + 1) * each)
        turned.append(
            call(partial(renorm_back_kernel, i * each * piece), [turn_part] * 2, placed[-1], *arrived[at], *own[at], *updates[at], name="renorm_back")
        )
    turn, direct = [t[0] for t in turned], [t[1] for t in turned]
    packed = [((end - start, width), f32) for start, end in cuts(3 * rows + 8, BACK_SETS)]

    def back_at(step, turned, before, first=False):
        outs = packed + [token_f32, token_f32]
        outs = call(
            partial(update_back_kernel, factor, order, step, first), outs, keys, values, log_rate, placed[step], direct_parts[step], gain_one, gain_two,
            *turned, *before, name="update_back",
        )
        return outs[:BACK_SETS], outs[BACK_SETS:]

    own, sums = back_at(chunks - 1, turn, direct, first=True)
    totals, held = None, turn
    for step in range(chunks - 1):
        held = [send(h) for h in held]
        mine_now, sums = back_at(step, held, sums)
        totals = [send(m if totals is None else totals[i] + m) for i, m in enumerate(mine_now)]
    grad_query, grad_key, grad_value, grad_rate = call(
        token_kernel, [((2, tokens, width), bf16), token_bf16, token_bf16, ((1, tokens), f32)],
        *sums, values, grad_gate_one, grad_up_one, old_weights, grad_gate_two, grad_up_two, new_weights, name="tokens",
    )
    grad_weights, grad_gain = call(finish_kernel, [chunk, ((1, width // chunks), f32)], *totals, *own, name="finish")
    return grad_query[:, :, None, :], grad_key[:, None, :], grad_value[:, None, :], grad_rate, grad_weights[None], grad_gain


def solution(mesh):
    placed = (
        P(None, "ctx", "head", None),
        P("ctx", "head", None),
        P("ctx", "head", None),
        P("head", "ctx"),
        P("head", None, None, None),
        P("head", None),
        P(None, "ctx", "head", None),
    )
    return jax.shard_map(
        partial(local, mesh.shape["ctx"], mesh.shape["head"]),
        mesh=mesh,
        in_specs=placed,
        out_specs=(
            P(None, "ctx", "head", None),
            P("ctx", "head", None),
            P("ctx", "head", None),
            P("head", "ctx"),
            P("head", None, "ctx", None),
            P("head", "ctx"),
        ),
        check_vma=False,
    )
```

```python
from functools import partial

import jax
import jax.numpy as jnp
from jax import lax
from jax.experimental import pallas as pl
from jax.experimental.pallas import tpu as pltpu
from jax.sharding import PartitionSpec as P

EPSILON = 1e-06
VMEM_BYTES = 16 * 1024 * 1024
SETS, TURN_SETS, BACK_SETS = 4, 2, 1
FIRST_VMEM, REST_VMEM = 60 * 1024 * 1024, 16 * 1024 * 1024
f32, bf16 = jnp.float32, jnp.bfloat16


def ring_order(count):
    width = max(w for w in range(1, count + 1) if count % w == 0 and w * w <= count)
    height = count // width
    if width == 1 or height % 2:
        return list(range(count))
    order = [0]
    for row in range(height):
        columns = range(1, width) if row % 2 == 0 else range(width - 1, 0, -1)
        order += [row * width + column for column in columns]
    return order + [row * width for row in range(height - 1, 0, -1)]


def ring_pairs(count, heads):
    order, pairs = ring_order(count), []
    for head in range(heads):
        way = order if head % 2 == 0 else order[::-1]
        pairs += [(way[at] * heads + head, way[(at + 1) % count] * heads + head) for at in range(count)]
    return pairs


def owner_at(order, step):
    device, sign = lax.axis_index("ctx"), 1 - 2 * lax.rem(lax.axis_index("head"), 2)
    count = len(order)
    at = sum(jnp.where(device == name, place, 0) for place, name in enumerate(order))
    place = lax.rem(at - sign * (1 + step) + 2 * count, count)
    return sum(jnp.where(place == i, name, 0) for i, name in enumerate(order))


def cuts(rows, sets):
    tiles = rows // 8
    ends = [8 * (tiles * (i + 1) // sets) for i in range(sets)]
    return list(zip([0] + ends[:-1], ends))


def pair(x):
    high = x.astype(bf16)
    return high, (x - high.astype(f32)).astype(bf16)


def nt(a, b):
    return lax.dot_general(a, b, (((1,), (1,)), ((), ())), preferred_element_type=f32)


def nn(a, b):
    return lax.dot_general(a, b, (((1,), (0,)), ((), ())), preferred_element_type=f32)


def tn(a, b):
    return lax.dot_general(a, b, (((0,), (0,)), ((), ())), preferred_element_type=f32)


def three(dot, a, b):
    (a_high, a_low), (b_high, b_low) = a, b
    return dot(a_high, b_high) + (dot(a_high, b_low) + dot(a_low, b_high))


def rows_by(x, mats):
    pairs = [pair(m) for m in mats]
    stacked = jnp.concatenate([p[0] for p in pairs] + [p[1] for p in pairs], axis=0)
    both = nt(x, stacked)
    half = both.shape[1] // 2
    total = both[:, :half] + both[:, half:]
    rows = mats[0].shape[0]
    return [total[:, i * rows : (i + 1) * rows] for i in range(len(mats))]


def sums_by(parts, x):
    pairs = [pair(m) for m in parts]
    stacked = jnp.concatenate([p[0] for p in pairs] + [p[1] for p in pairs], axis=1)
    both = tn(stacked, x)
    half = both.shape[0] // 2
    total = both[:half] + both[half:]
    rows = parts[0].shape[1]
    return [total[i * rows : (i + 1) * rows] for i in range(len(parts))]


def silu_parts(gate):
    sig = 1.0 / (1.0 + jnp.exp(-gate))
    act = gate * sig
    return sig, act, sig + act * (1.0 - sig)


def to_columns(rows):
    count, tokens = rows.shape
    if count < 128:
        rows = jnp.concatenate([rows, jnp.zeros((128 - count, tokens), f32)], axis=0)
    turned = jnp.transpose(rows)
    return [turned[:, i : i + 1] for i in range(count)]


def to_rows(columns):
    tokens = columns[0].shape[0]
    lane = lax.broadcasted_iota(jnp.int32, (tokens, 128), 1)
    packed = jnp.zeros((tokens, 128), f32)
    for i, column in enumerate(columns):
        packed = jnp.where(lane == i, column, packed)
    return jnp.transpose(packed)[:8]


def minus_rate(rate_ref, factor):
    return -jnp.exp(to_columns(rate_ref[...])[0]) * factor


def write_parts(parts_ref, sums, steps):
    piece = sums[0].shape[0] // steps // SETS
    for at, part_ref in enumerate(parts_ref):
        for i, total in enumerate(sums):
            part_ref[i] = total[at * piece : (at + 1) * piece]


def update_kernel(factor, order, first, steps, weights_ref, key_ref, value_ref, rate_ref, *refs):
    placed_ref, key_here, value_here, weight_sems, token_sems = refs[-5:]
    parts_ref, chunks_ref = refs[: SETS * steps], refs[SETS * steps : -5]
    rows = weights_ref.shape[1] // len(order)
    copies = [pltpu.make_async_copy(key_ref, key_here, token_sems.at[0])]
    copies[0].start()
    for step in range(steps):
        source = weights_ref.at[:, pl.ds(pl.multiple_of(owner_at(order, first + step) * rows, rows), rows), :]
        copy = pltpu.make_async_copy(source, placed_ref.at[:, pl.ds(step * rows, rows), :], weight_sems.at[step])
        copy.start()
        copies.append(copy)
    copy = pltpu.make_async_copy(value_ref, value_here, token_sems.at[1])
    copy.start()
    rate = minus_rate(rate_ref, factor)
    for copy in copies + [copy]:
        copy.wait()
    keys, values = key_here[...], value_here[...]
    gate, up = rows_by(keys, [placed_ref[0], placed_ref[1]])
    (back,) = rows_by(values, [placed_ref[2]])
    _, act, slope = silu_parts(gate)
    back = back * rate
    grad_gate, grad_up = sums_by([back * up * slope, back * act], keys)
    (grad_down,) = sums_by([act * up * rate], values)
    write_parts(parts_ref, [grad_gate, grad_up, grad_down], steps)
    for step, chunk_ref in enumerate(chunks_ref):
        chunk_ref[...] = placed_ref[:, step * rows : (step + 1) * rows, :]


def scales(update, anchor):
    target = jnp.sqrt(jnp.sum(anchor * anchor, axis=-1, keepdims=True) + EPSILON)
    actual = jnp.sqrt(jnp.sum(update * update, axis=-1, keepdims=True) + EPSILON)
    return target, actual


def renorm_kernel(start, arrived_ref, mine_ref, anchor_ref, update_ref, new_ref):
    anchor = anchor_ref[:, start : start + update_ref.shape[1], :]
    update = anchor - (arrived_ref[...] + mine_ref[...])
    target, actual = scales(update, anchor)
    update_ref[...] = update
    new_ref[...] = update * (target / actual)


def renorm_back_kernel(start, anchor_ref, *refs):
    sets, (turned_ref, direct_ref) = (len(refs) - 2) // 3, refs[-2:]
    piece = refs[0].shape[1]
    for i in range(sets):
        at = slice(i * piece, (i + 1) * piece)
        anchor = anchor_ref[:, start + i * piece : start + (i + 1) * piece, :]
        cot, update = refs[i][...] + refs[sets + i][...], refs[2 * sets + i][...]
        target, actual = scales(update, anchor)
        inner = jnp.sum(update * cot, axis=-1, keepdims=True)
        ratio = target / actual
        update_cot = ratio * cot - update * (inner * ratio / (actual * actual))
        turned_ref[:, at, :] = -update_cot
        direct_ref[:, at, :] = update_cot + anchor * (inner / (actual * target))


def forward_pass(queries, gate_mat, up_mat, down_mat):
    gate, up = rows_by(queries, [gate_mat, up_mat])
    _, act, _ = silu_parts(gate)
    out = three(nn, pair(act * up), pair(down_mat))
    return gate, up, out


def norm_sums(out, cotan, gain):
    return [jnp.sum(out * out, axis=1, keepdims=True), jnp.sum(gain * cotan * out, axis=1, keepdims=True)]


def forward_kernel(count, other, query_ref, cotan_ref, gain_ref, *refs):
    if other:
        other_ref, refs = refs[0], refs[1:]
    chunks, (weights_ref, gate_ref, up_ref, out_ref, stats_ref) = refs[:count], refs[count:]
    rows = weights_ref.shape[1] // count
    for i, chunk in enumerate(chunks):
        weights_ref[:, i * rows : (i + 1) * rows, :] = chunk[...]
    gate, up, out = forward_pass(query_ref[...], weights_ref[0], weights_ref[1], weights_ref[2])
    gate_ref[...] = gate
    up_ref[...] = up
    out_ref[...] = out
    sums = norm_sums(out, cotan_ref[...].astype(f32), gain_ref[...])
    if other:
        stats_ref[...] = to_rows([jnp.zeros((out.shape[0], 1), f32)] * 2 + sums) + other_ref[...]
    else:
        stats_ref[...] = to_rows(sums)


def out_cotangent(first, width, cotan_ref, gain_ref, stats_ref, out_ref):
    columns = to_columns(stats_ref[...])
    square, product = columns[first], columns[first + 1]
    inverse = 1.0 / jnp.sqrt(square / width + EPSILON)
    out, cotan = out_ref[...], cotan_ref[...].astype(f32)
    grad_out = gain_ref[...] * cotan * inverse - out * (inverse * inverse * inverse * product / width)
    return pair(grad_out), jnp.sum(cotan * out * inverse, axis=0, keepdims=True)


def backward_sums(queries, grad_out, gate, up, down_mat):
    _, act, slope = silu_parts(gate)
    back = three(nt, grad_out, pair(down_mat))
    grad_gate, grad_up = back * up * slope, back * act
    return grad_gate, grad_up, sums_by([grad_gate, grad_up], queries) + [three(tn, pair(act * up), grad_out)]


def backward_kernel(first, width, chunks, split, query_ref, cotan_ref, gain_ref, stats_ref, weights_ref, gate_ref, up_ref, out_ref, grad_gate_ref, grad_up_ref, gain_term_ref, *parts_ref):
    grad_out, gain_term_ref[...] = out_cotangent(first, width, cotan_ref, gain_ref, stats_ref, out_ref)
    grad_gate_ref[...], grad_up_ref[...], sums = backward_sums(query_ref[...], grad_out, gate_ref[...], up_ref[...], weights_ref[2])
    rows = sums[0].shape[0] // chunks
    if split:
        write_parts(parts_ref, sums, chunks)
    else:
        for step in range(chunks):
            for i, total in enumerate(sums):
                parts_ref[step][i] = total[step * rows : (step + 1) * rows]


def token_kernel(key_sum_ref, value_sum_ref, value_ref, *refs):
    blocks, (grad_query_ref, grad_key_ref, grad_value_ref, grad_rate_ref) = refs[:-4], refs[-4:]
    grad_value = value_sum_ref[...]
    grad_rate_ref[...] = to_rows([jnp.sum(grad_value * value_ref[...].astype(f32), axis=1, keepdims=True)])[:1]
    grad_key_ref[...] = key_sum_ref[...].astype(bf16)
    grad_value_ref[...] = grad_value.astype(bf16)
    for block in range(2):
        grad_gate_ref, grad_up_ref, weights_ref = blocks[3 * block : 3 * block + 3]
        total = three(nn, pair(grad_gate_ref[...]), pair(weights_ref[0]))
        total = total + three(nn, pair(grad_up_ref[...]), pair(weights_ref[1]))
        grad_query_ref[block] = total.astype(bf16)


def second_order(keys, values, rate, weights, turns):
    gate, up, gate_turn, up_turn = rows_by(keys, [weights[0], weights[1], turns[0], turns[1]])
    back, back_turn = rows_by(values, [weights[2], turns[2]])
    back, back_turn = back * rate, back_turn * rate
    sig, act, slope = silu_parts(gate)
    bend = sig * (1.0 - sig) * (2.0 + gate * (1.0 - 2.0 * sig))
    hidden_turn = slope * gate_turn * up + act * up_turn
    cot_gate = back * (bend * gate_turn * up + slope * up_turn) + back_turn * up * slope
    cot_up = back * slope * gate_turn + back_turn * act
    return act * up, hidden_turn, cot_gate, cot_up, back * slope * up, back * act


def update_back_kernel(factor, order, step, first, key_ref, value_ref, rate_ref, weights_ref, gathered_ref, gain_one_ref, gain_two_ref, *refs):
    turns_ref, refs = refs[:TURN_SETS], refs[TURN_SETS:]
    if first:
        direct_ref, refs = refs[:TURN_SETS], refs[TURN_SETS:]
    else:
        before_key_ref, before_value_ref, refs = refs[0], refs[1], refs[2:]
    outs_ref, (grad_key_ref, grad_value_ref) = refs[:BACK_SETS], refs[BACK_SETS:]
    keys, values = key_ref[...], value_ref[...]
    rate = minus_rate(rate_ref, factor)
    weights, turns = [weights_ref[i] for i in range(3)], [jnp.concatenate([t[i] for t in turns_ref], axis=0) for i in range(3)]
    hidden, hidden_turn, cot_gate, cot_up, cot_gate_turn, cot_up_turn = second_order(keys, values, rate, weights, turns)
    sums = sums_by([cot_gate, cot_up], keys) + sums_by([hidden_turn * rate], values)
    sums = [total + gathered_ref[i] for i, total in enumerate(sums)]
    if first:
        sums = [total + jnp.concatenate([d[i] for d in direct_ref], axis=0) for i, total in enumerate(sums)]
    gain = jnp.broadcast_to(gain_one_ref[...] + gain_two_ref[...], (8, gain_one_ref.shape[1]))
    piece = gain.shape[1] // len(order)
    sums.append(pltpu.roll(gain, lax.rem((len(order) - owner_at(order, step)) * piece, gain.shape[1]), 1))
    packed, at = jnp.concatenate(sums, axis=0), 0
    for out_ref in outs_ref:
        out_ref[...] = packed[at : at + out_ref.shape[0]]
        at += out_ref.shape[0]
    grad_key = three(nn, pair(jnp.concatenate([cot_gate, cot_up, cot_gate_turn, cot_up_turn], axis=1)), pair(jnp.concatenate([weights[0], weights[1], turns[0], turns[1]], axis=0)))
    grad_value = rate * three(nn, pair(jnp.concatenate([hidden_turn, hidden], axis=1)), pair(jnp.concatenate([weights[2], turns[2]], axis=0)))
    if not first:
        grad_key, grad_value = grad_key + before_key_ref[...], grad_value + before_value_ref[...]
    grad_key_ref[...] = grad_key
    grad_value_ref[...] = grad_value


def finish_kernel(*refs):
    arrived, mine, (weights_ref, gain_ref) = refs[:BACK_SETS], refs[BACK_SETS : 2 * BACK_SETS], refs[2 * BACK_SETS :]
    rows = weights_ref.shape[1]
    total = jnp.concatenate([a[...] + m[...] for a, m in zip(arrived, mine)], axis=0)
    for i in range(3):
        weights_ref[i] = total[i * rows : (i + 1) * rows]
    gain_ref[...] = total[3 * rows : 3 * rows + 1, : gain_ref.shape[1]]


def call(kernel, outs, *args, in_hbm=0, scratch=(), name=None, micros=4, vmem=VMEM_BYTES):
    in_specs = [pl.BlockSpec(memory_space=pl.ANY)] * in_hbm + [pl.BlockSpec(memory_space=pltpu.VMEM)] * (len(args) - in_hbm)
    return pl.pallas_call(
        kernel,
        out_shape=[jax.ShapeDtypeStruct(shape, dtype) for shape, dtype in outs],
        in_specs=in_specs,
        out_specs=[pl.BlockSpec(memory_space=pltpu.VMEM)] * len(outs),
        scratch_shapes=scratch,
        compiler_params=pltpu.CompilerParams(vmem_limit_bytes=vmem),
        cost_estimate=pl.CostEstimate(flops=int(micros * 1e9), transcendentals=0, bytes_accessed=int(micros * 3e6)),
        name=name,
    )(*args)


def local(chunks, heads, query_tokens, key_tokens, value_tokens, log_rate, fast_weights, norm_gain, out_grad):
    order, pairs = ring_order(chunks), ring_pairs(chunks, heads)

    def send(x):
        return lax.ppermute(x, ("ctx", "head"), pairs)

    weights = fast_weights[0]
    query_one, query_two = query_tokens[0, :, 0, :], query_tokens[1, :, 0, :]
    cotan_one, cotan_two = out_grad[0, :, 0, :], out_grad[1, :, 0, :]
    keys, values = key_tokens[:, 0, :], value_tokens[:, 0, :]
    tokens, width = keys.shape
    hidden = weights.shape[1]
    rows = hidden // chunks
    factor = (tokens * chunks * width) ** (-0.5)
    norm_width = heads * width
    token_f32, token_bf16, whole = ((tokens, width), f32), ((tokens, width), bf16), ((3, hidden, width), f32)
    hidden_f32, stats_shape, gain_shape = ((tokens, hidden), f32), ((8, tokens), f32), ((1, width), f32)
    piece = rows // SETS
    chunk, part, turn_part = ((3, rows, width), f32), ((3, piece, width), f32), ((3, rows // TURN_SETS, width), f32)

    def scatter(parts):
        totals = list(parts[:SETS])
        for step in range(chunks - 1):
            totals = [send(t) for t in totals]
            if step < chunks - 2:
                totals = [t + p for t, p in zip(totals, parts[SETS * (step + 1) :])]
        return totals

    def update(first, steps, keep, vmem):
        return call(
            partial(update_kernel, factor, order, first, steps), [part] * (SETS * steps) + ([chunk] * steps if keep else []), weights, keys, values, log_rate,
            in_hbm=3, vmem=vmem, name="update",
            scratch=[pltpu.VMEM((3, steps * rows, width), f32), pltpu.VMEM((tokens, width), bf16), pltpu.VMEM((tokens, width), bf16)]
            + [pltpu.SemaphoreType.DMA((steps,)), pltpu.SemaphoreType.DMA((2,))],
        )

    parts = update(0, 1, True, FIRST_VMEM)
    parts, placed = parts[:SETS], parts[SETS:]
    rest = update(1, chunks - 1, True, REST_VMEM)
    parts, placed = parts + rest[: -(chunks - 1)], placed + rest[-(chunks - 1) :]
    arrived = scatter(parts)
    old_weights, gate_one, up_one, out_one, stats_one = call(
        partial(forward_kernel, chunks, False), [whole, hidden_f32, hidden_f32, token_f32, stats_shape], query_one, cotan_one, norm_gain, *placed, name="forward_one"
    )
    updates, gathered = [], []
    for i in range(SETS):
        new = call(partial(renorm_kernel, i * piece), [part] * 2, arrived[i], parts[i - SETS], placed[-1], name="renorm")
        updates.append(new[0])
        gathered.append(new[1])
    held, gathered = gathered, []
    news = held
    for step in range(chunks - 1):
        held = [send(h) for h in held]
        gathered += held
    gathered += news

    new_weights, gate_two, up_two, out_two, stats = call(
        partial(forward_kernel, len(gathered), True), [whole, hidden_f32, hidden_f32, token_f32, stats_shape],
        query_two, cotan_two, norm_gain, stats_one, *gathered, name="forward_two",
    )
    if heads <= 4:
        others = [lax.ppermute(stats, "head", [(i, (i + d) % heads) for i in range(heads)]) for d in range(1, heads)]
        stats = sum(others, stats)
    else:
        stats = lax.psum(stats, "head")
    grad_gate_two, grad_up_two, gain_two, *parts = call(
        partial(backward_kernel, 2, norm_width, chunks, True), [hidden_f32, hidden_f32, gain_shape] + [part] * (SETS * chunks),
        query_two, cotan_two, norm_gain, stats, new_weights, gate_two, up_two, out_two, name="backward_two",
    )
    arrived = scatter(parts)
    grad_gate_one, grad_up_one, gain_one, *direct_parts = call(
        partial(backward_kernel, 0, norm_width, chunks, False), [hidden_f32, hidden_f32, gain_shape] + [chunk] * chunks,
        query_one, cotan_one, norm_gain, stats, old_weights, gate_one, up_one, out_one, name="backward_one",
    )

    own, turned, each = parts[-SETS:], [], SETS // TURN_SETS
    for i in range(TURN_SETS):
        at = slice(i * each, (i + 1) * each)
        turned.append(
            call(partial(renorm_back_kernel, i * each * piece), [turn_part] * 2, placed[-1], *arrived[at], *own[at], *updates[at], name="renorm_back")
        )
    turn, direct = [t[0] for t in turned], [t[1] for t in turned]
    packed = [((end - start, width), f32) for start, end in cuts(3 * rows + 8, BACK_SETS)]

    def back_at(step, turned, before, first=False):
        outs = packed + [token_f32, token_f32]
        outs = call(
            partial(update_back_kernel, factor, order, step, first), outs, keys, values, log_rate, placed[step], direct_parts[step], gain_one, gain_two,
            *turned, *before, name="update_back",
        )
        return outs[:BACK_SETS], outs[BACK_SETS:]

    own, sums = back_at(chunks - 1, turn, direct, first=True)
    totals, held = None, turn
    for step in range(chunks - 1):
        held = [send(h) for h in held]
        mine_now, sums = back_at(step, held, sums)
        totals = [send(m if totals is None else totals[i] + m) for i, m in enumerate(mine_now)]
    grad_query, grad_key, grad_value, grad_rate = call(
        token_kernel, [((2, tokens, width), bf16), token_bf16, token_bf16, ((1, tokens), f32)],
        *sums, values, grad_gate_one, grad_up_one, old_weights, grad_gate_two, grad_up_two, new_weights, name="tokens",
    )
    grad_weights, grad_gain = call(finish_kernel, [chunk, ((1, width // chunks), f32)], *totals, *own, name="finish")
    return grad_query[:, :, None, :], grad_key[:, None, :], grad_value[:, None, :], grad_rate, grad_weights[None], grad_gain


def solution(mesh):
    placed = (
        P(None, "ctx", "head", None),
        P("ctx", "head", None),
        P("ctx", "head", None),
        P("head", "ctx"),
        P("head", None, None, None),
        P("head", None),
        P(None, "ctx", "head", None),
    )
    return jax.shard_map(
        partial(local, mesh.shape["ctx"], mesh.shape["head"]),
        mesh=mesh,
        in_specs=placed,
        out_specs=(
            P(None, "ctx", "head", None),
            P("ctx", "head", None),
            P("ctx", "head", None),
            P("head", "ctx"),
            P("head", None, "ctx", None),
            P("head", "ctx"),
        ),
        check_vma=False,
    )
```
